32 devices in a mesh: head: 8 (over z, x), dp: 4 (over y, core).
Axes of the slice: x: 2, y: 2, z: 4, core: 2. Of those that a mesh axis runs over, the one named last changes fastest.
Arguments:
- tokens: bfloat16 [8192, 1024], P('dp'), may hold values from -6 to 6
- cotangent: bfloat16 [8192, 1024], P('dp'), may hold values from -6 to 6
- group_ids: int32 [4], P('dp'), may hold values from 0 to 7
- group_weights: float32 [8], replicated, may hold values from 0.25 to 2
- gain_attn: float32 [1024], replicated, may hold values from 0.5 to 1.5
- w_query: bfloat16 [1024, 1024], P(None, 'head'), may hold values from -0.1875 to 0.1875
- w_latent: bfloat16 [1024, 512], replicated, may hold values from -0.1875 to 0.1875
- w_key: bfloat16 [256, 1024], P(None, 'head'), may hold values from -0.375 to 0.375
- w_value: bfloat16 [256, 1024], P(None, 'head'), may hold values from -0.375 to 0.375
- w_out: bfloat16 [1024, 1024], P('head'), may hold values from -1.5 to 1.5
- gain_mlp: float32 [1024], replicated, may hold values from 0.5 to 1.5
- w_gate: bfloat16 [1024, 2816], P(None, 'head'), may hold values from -0.1875 to 0.1875
- w_up: bfloat16 [1024, 2816], P(None, 'head'), may hold values from -0.1875 to 0.1875
- w_down: bfloat16 [2816, 1024], P('head'), may hold values from -0.109375 to 0.109375
Outputs:
- block_out: bfloat16 [8192, 1024], P('dp')
- grad_tokens: bfloat16 [8192, 1024], P('dp')
- grad_gain_attn: float32 [1024], P('dp')
- grad_w_query: float32 [1024, 1024], P('dp', 'head')
- grad_w_latent: float32 [1024, 512], P('dp', 'head')
- grad_w_key: float32 [256, 1024], P('dp', 'head')
- grad_w_value: float32 [256, 1024], P('dp', 'head')
- grad_w_out: float32 [1024, 1024], P('head', 'dp')
- grad_gain_mlp: float32 [1024], P('dp')
- grad_w_gate: float32 [1024, 2816], P('dp', 'head')
- grad_w_up: float32 [1024, 2816], P('dp', 'head')
- grad_w_down: float32 [2816, 1024], P('head', 'dp')
The draws below stay inside these ranges and needn't reach their ends.
All inputs are finite; a program needn't handle non-finite values.
Results may differ from the reference program's by a relative error of at most 0.025.
Values may be sent and summed in bfloat16 or wider, within the bound.
No kernel may reach another device: no remote copies, remote signals or barrier semaphores. Data moves between devices by JAX's collectives and lax.ppermute only.
A program may use at most 192 MiB of HBM per device.

```python
import math
import jax
import jax.numpy as jnp
import numpy as np
from jax import lax

D = 1024
H = 16
HD = 64
LAT = 256
FF = 2816
SEQ_LEN = 2048
GROUPS = 8
ROWS = 4
TOKENS = 8192
N_HEAD = 8


def place_ends(drawn, key, smallest, largest):
    shape = drawn.shape
    spot = [jax.random.randint(jax.random.fold_in(key, axis), (), 0, shape[axis]) for axis in range(len(shape))]
    drawn = drawn.at[tuple(spot)].set(smallest)
    longest = shape.index(max(shape))
    spot[longest] = (spot[longest] + 1) % shape[longest]
    return drawn.at[tuple(spot)].set(largest)


def spiked(values, stream_key, source, target, parts, factor):
    owner, partner = [(jnp.arange(values.shape[dim]) // (values.shape[dim] // parts)).reshape([-1 if axis == dim else 1 for axis in range(values.ndim)]) for dim in (source, target)]
    chosen = jax.random.permutation(stream_key, parts)[partner]
    strong = (owner == chosen) | (owner == (partner + parts // 2) % parts)
    return jnp.where(strong, factor * values, values)


def levels(key, shape, cuts, low, largest):
    level, own = 1.0, jax.random.fold_in(key, 6)
    for dim, shards_of in cuts:
        draws = jnp.exp(jax.random.uniform(jax.random.fold_in(own, dim), (shards_of,), jnp.float32, low / len(cuts), largest / len(cuts)))
        level = level * jnp.repeat(draws, shape[dim] // shards_of).reshape([-1 if axis == dim else 1 for axis in range(len(shape))])
    return level


def rank_bounds(number_of, lean):
    weights = [(1 << 20) // math.isqrt(grade ** lean) + 1 for grade in range(1, number_of + 1)]
    scale = 1 + sum(weights) // (1 << 30)
    return np.cumsum(np.array([max(1, weight // scale) for weight in weights]))


def ranked_ids(own_key, dims, count, skew):
    grid = rank_bounds(count, skew)
    pick = jax.random.randint(jax.random.fold_in(own_key, 1), dims, 0, int(grid[count - 1]))
    grade = jnp.searchsorted(jnp.asarray(grid, jnp.int32), pick, side="right")
    return jax.random.permutation(jax.random.fold_in(own_key, 2), count)[grade].astype(jnp.int32)


def gaussian(own_key, shape, scale, limit, pieces=(), kind=jnp.bfloat16):
    level = levels(own_key, shape, pieces, -0.22, 0.18) if pieces else 1.0
    entries = jax.random.normal(own_key, shape, jnp.float32) * scale * level
    return jnp.minimum(jnp.maximum(entries, -limit), limit).astype(kind)


def noise_with(rng, dims, deviation, limit, shards, heavy, kind=jnp.bfloat16):
    result = deviation * jax.random.normal(rng, dims, jnp.float32)
    if shards:
        result = result * levels(rng, dims, shards, -0.22, 0.18)
    return jnp.clip(spiked(result, jax.random.fold_in(rng, 3), *heavy), -limit, limit).astype(kind)


def setup_inputs(seed: int = 0) -> dict:
    streams_of = jax.random.split(jax.random.key(seed), 15)
    return {
        "tokens": gaussian(streams_of[0], (TOKENS, D), 1.0, 6.0, ((0, 4),)),
        "cotangent": noise_with(streams_of[1], (TOKENS, D), 1.0, 6.0, ((0, 4),), (0, 1, 4, 2.0)),
        "group_ids": place_ends(ranked_ids(streams_of[2], (ROWS,), GROUPS, 2), jax.random.fold_in(streams_of[2], 3), 0, GROUPS - 1).astype(jnp.int32),
        "group_weights": jnp.clip(jnp.exp(jax.random.uniform(streams_of[3], (GROUPS,), jnp.float32, math.log(0.25), math.log(2.0))), 0.25, 2.0),
        "gain_attn": jnp.clip(1.0 + 0.1 * jax.random.normal(streams_of[4], (D,), jnp.float32), 0.5, 1.5),
        "w_query": gaussian(streams_of[5], (D, H * HD), D ** -0.5, 0.1875, ((1, 8),)),
        "w_latent": gaussian(streams_of[6], (D, 2 * LAT), D ** -0.5, 0.1875),
        "w_key": gaussian(streams_of[7], (LAT, H * HD), LAT ** -0.5, 0.375, ((1, 8),)),
        "w_value": gaussian(streams_of[8], (LAT, H * HD), LAT ** -0.5, 0.375, ((1, 8),)),
        "w_out": gaussian(streams_of[9], (H * HD, D), (H * HD // 64) ** -0.5, 1.5, ((0, 8),)),
        "gain_mlp": jnp.clip(1.0 + 0.1 * jax.random.normal(streams_of[10], (D,), jnp.float32), 0.5, 1.5),
        "w_gate": gaussian(streams_of[11], (D, FF), D ** -0.5, 0.1875, ((1, 8),)),
        "w_up": gaussian(streams_of[12], (D, FF), D ** -0.5, 0.1875, ((1, 8),)),
        "w_down": gaussian(streams_of[13], (FF, D), FF ** -0.5, 0.109375, ((0, 8),)),
    }


epsilon = 1e-05
negative = -1e+30
highest_precision = lax.Precision.HIGHEST

@jax.custom_vjp
def reduced_precision(v):
    return lax.optimization_barrier(v.astype(jnp.bfloat16)).astype(jnp.float32)

@jax.custom_vjp
def low_back(v):
    return v

def low_keep(v):
    return (reduced_precision(v), None)

def low_pass(kept, grad):
    return (grad,)

def back_keep(v):
    return (v, None)

def back_low(kept, grad):
    return (reduced_precision(grad),)
reduced_precision.defvjp(low_keep, low_pass)
low_back.defvjp(back_keep, back_low)

def rms_gain(values_in, gain_vec):
    return values_in * lax.rsqrt(lax.optimization_barrier(jnp.mean(values_in * values_in, axis=-1, keepdims=True)) + epsilon) * gain_vec

def attention(query_all, key_all, value_all):
    length = query_all.shape[1]
    block_rows = min(512, length)
    block_count = length // block_rows

    def per_block(first_row):
        query_block = lax.dynamic_slice_in_dim(query_all, first_row, block_rows, 1)
        raw_scores = jnp.einsum('hqe,hke->hqk', query_block, key_all, precision=highest_precision)
        scores = low_back(raw_scores) * HD ** (-0.5)
        row_ids = first_row + jnp.arange(block_rows, dtype=jnp.int32)[:, None]
        col_ids = jnp.arange(length, dtype=jnp.int32)[None, :]
        scores = jnp.where((col_ids <= row_ids)[None], scores, negative)
        weights = reduced_precision(jax.nn.softmax(scores, axis=-1))
        return jnp.einsum('hqk,hke->hqe', weights, value_all, precision=highest_precision)
    starts = jnp.arange(block_count, dtype=jnp.int32) * block_rows
    outputs = lax.map(jax.checkpoint(per_block), starts)
    return outputs.transpose(1, 0, 2, 3).reshape(query_all.shape)

def layer(inputs, gain_attn, w_query, w_latent, w_key, w_value, w_out, gain_mlp, w_gate, w_up, w_down):
    groups = N_HEAD
    per_group = H // N_HEAD
    length = inputs.shape[0]
    normed = reduced_precision(rms_gain(inputs, gain_attn))
    replica_count = low_back(jnp.broadcast_to(normed[None], (groups, length, D)))
    query_w = w_query.reshape(D, groups, per_group * HD).transpose(1, 0, 2)
    queries = low_back(reduced_precision(jnp.einsum('gld,gde->gle', replica_count, query_w, precision=highest_precision)))
    latent_ids = jnp.arange(groups, dtype=jnp.int32) // (groups // 2)
    latent_weight = w_latent.reshape(D, 2, LAT)[:, latent_ids, :].transpose(1, 0, 2)
    latent_state = reduced_precision(jnp.einsum('ebz,ezt->ebt', replica_count, latent_weight, precision=highest_precision))
    per_head = low_back(jnp.broadcast_to(latent_state[:, None], (groups, per_group, length, LAT)))
    key_w = w_key.reshape(LAT, groups, per_group, HD).transpose(1, 2, 0, 3)
    value_w = w_value.reshape(LAT, groups, per_group, HD).transpose(1, 2, 0, 3)
    keys = low_back(reduced_precision(jnp.einsum('gplc,gpce->gple', per_head, key_w, precision=highest_precision)))
    values = low_back(reduced_precision(jnp.einsum('gplc,gpce->gple', per_head, value_w, precision=highest_precision)))
    query_heads = queries.reshape(groups, length, per_group, HD).transpose(0, 2, 1, 3).reshape(H, length, HD)
    mixed = attention(query_heads, keys.reshape(H, length, HD), values.reshape(H, length, HD))
    mixed = low_back(reduced_precision(mixed))
    mixed_groups = mixed.reshape(groups, per_group, length, HD).transpose(0, 2, 1, 3).reshape(groups, length, per_group * HD)
    out_w = w_out.reshape(groups, per_group * HD, D)
    attn_parts = reduced_precision(low_back(jnp.einsum('gle,ged->gld', mixed_groups, out_w, precision=highest_precision)))
    hidden_state = inputs + lax.optimization_barrier(jnp.sum(attn_parts, axis=0))
    normed2 = reduced_precision(rms_gain(hidden_state, gain_mlp))
    copies2 = low_back(jnp.broadcast_to(normed2[None], (groups, length, D)))
    cols_group = FF // groups
    gate_matrix = w_gate.reshape(D, groups, cols_group).transpose(1, 0, 2)
    up_w = w_up.reshape(D, groups, cols_group).transpose(1, 0, 2)
    gate_proj = low_back(jnp.einsum('gld,gdf->glf', copies2, gate_matrix, precision=highest_precision))
    up_proj = low_back(jnp.einsum('gld,gdf->glf', copies2, up_w, precision=highest_precision))
    activated = reduced_precision(jax.nn.silu(gate_proj) * up_proj)
    down_w = w_down.reshape(groups, cols_group, D)
    mlp_parts = reduced_precision(low_back(jnp.einsum('glf,gfd->gld', activated, down_w, precision=highest_precision)))
    return hidden_state + lax.optimization_barrier(jnp.sum(mlp_parts, axis=0))

def reference(tokens, cotangent, group_ids, group_weights, gain_attn, w_query, w_latent, w_key, w_value, w_out, gain_mlp, w_gate, w_up, w_down):
    params = tuple((member.astype(jnp.float32) for member in (gain_attn, w_query, w_latent, w_key, w_value, w_out, gain_mlp, w_gate, w_up, w_down)))
    inputs = tokens.astype(jnp.float32).reshape(ROWS, SEQ_LEN, D)
    grads_in = cotangent.astype(jnp.float32).reshape(ROWS, SEQ_LEN, D)
    labels = jnp.arange(GROUPS, dtype=jnp.int32)
    row_weight = lax.optimization_barrier(jnp.sum(jnp.where(group_ids[:, None] == labels[None, :], group_weights.astype(jnp.float32)[None, :], 0.0), axis=1))

    def per_sequence(running, member):
        sequence, grad_seq, weight_row = member
        output, backward_function = jax.vjp(layer, sequence, *params)
        grads = backward_function(grad_seq * weight_row)
        running = tuple((summed + fresh for summed, fresh in zip(running, grads[1:])))
        return (running, (output, grads[0]))
    start_acc = tuple((jnp.zeros_like(member) for member in params))
    totals, (outputs, grad_inputs) = lax.scan(per_sequence, start_acc, (inputs, grads_in, row_weight))
    block_out = outputs.reshape(TOKENS, D).astype(jnp.bfloat16)
    grad_tokens = grad_inputs.reshape(TOKENS, D).astype(jnp.bfloat16)
    return (block_out, grad_tokens, totals[0], totals[1], totals[2], totals[3], totals[4], totals[5], totals[6], totals[7], totals[8], totals[9])
```

```python
import functools

import jax
import jax.numpy as jnp
from jax import lax
from jax.experimental import pallas as pl
from jax.experimental.pallas import tpu as pltpu
from jax.sharding import PartitionSpec as P

HD = 64
epsilon = 1e-05
negative = -1e30


def snake_order(count):
    return list(range(0, count, 2)) + list(range(count - 1, 0, -2))


class Ring:
    def __init__(self):
        self.count = lax.axis_size("head")
        order = snake_order(self.count)
        self.forward = [(order[i], order[(i + 1) % self.count]) for i in range(self.count)]
        self.backward = [(b, a) for a, b in self.forward]
        index = lax.axis_index("head")
        self.place = jnp.where(index % 2 == 0, index // 2, self.count - 1 - index // 2)

    def owner(self, offset):
        spot = (self.place + offset) % self.count
        half = self.count // 2
        return jnp.where(spot < half, 2 * spot, 2 * (self.count - 1 - spot) + 1)

    def gather(self, own):
        half = self.count // 2
        blocks = {0: own}
        ahead = behind = own
        for step in range(1, half):
            ahead = lax.ppermute(ahead, "head", self.forward)
            behind = lax.ppermute(behind, "head", self.backward)
            blocks[-step], blocks[step] = ahead, behind
        cut = own.shape[-1] // 2
        left = lax.ppermute(ahead[..., :cut], "head", self.forward)
        right = lax.ppermute(behind[..., cut:], "head", self.backward)
        blocks[half] = jnp.concatenate([left, right], axis=-1)
        return blocks

    def scatter(self, block):
        half = self.count // 2
        far = block(half)
        cut = far.shape[-1] // 2
        ahead = lax.ppermute(far[..., :cut], "head", self.forward)
        behind = lax.ppermute(far[..., cut:], "head", self.backward)
        for step in range(half - 1, 0, -1):
            give_ahead, give_behind = block(step), block(-step)
            if step == half - 1:
                give_ahead = jnp.concatenate(
                    [add(give_ahead[..., :cut], ahead), give_ahead[..., cut:]], axis=-1
                )
                give_behind = jnp.concatenate(
                    [give_behind[..., :cut], add(give_behind[..., cut:], behind)], axis=-1
                )
            else:
                give_ahead, give_behind = add(give_ahead, ahead), add(give_behind, behind)
            ahead = lax.ppermute(give_ahead, "head", self.forward)
            behind = lax.ppermute(give_behind, "head", self.backward)
        return wide(block(0)) + wide(ahead) + wide(behind)


def wide(block):
    return block.astype(jnp.float32)


def add(left, right):
    return (wide(left) + wide(right)).astype(jnp.bfloat16)


def flip(block, bit):
    count = lax.axis_size("dp")
    return lax.ppermute(block, "dp", [(i, i ^ bit) for i in range(count)])


def dp_gather(own):
    bits = lax.axis_size("dp").bit_length() - 1
    for bit in reversed(range(bits)):
        own = jnp.concatenate([own, flip(own, 1 << bit)], axis=0)
    return own


def dp_bit_order():
    bits = lax.axis_size("dp").bit_length() - 1
    order = [0]
    for bit in reversed(range(bits)):
        order = order + [r | 1 << bit for r in order]
    return order


def dp_scatter(blocks):
    bits = lax.axis_size("dp").bit_length() - 1
    for bit in range(bits):
        half = blocks.shape[0] // 2
        got = flip(blocks[half:], 1 << bit)
        if bit == bits - 1:
            return wide(blocks[:half]) + wide(got)
        blocks = add(blocks[:half], got)
    return wide(blocks)


def dot_last(a, b):
    return lax.dot_general(a, b, (((1,), (1,)), ((), ())), preferred_element_type=jnp.float32)

def dot_plain(a, b):
    return jnp.dot(a, b, preferred_element_type=jnp.float32)

def lane_heads(x, e):
    lane = lax.broadcasted_iota(jnp.int32, x.shape, 1)
    return jnp.where(lane // HD == e, x, jnp.zeros_like(x))

def segments(length, block):
    half = length // 2
    if block % 128 == 0:
        return ((0, half, 0, 2 * block, block), (half, length, block, 2 * block, block))
    return ((0, half, 0, 2 * block, 2 * block), (half, length, 0, 2 * block, 2 * block))

def visible(first_key, count, first_col, cols, block, rank, ranks):
    key = first_key + lax.broadcasted_iota(jnp.int32, (count, cols), 0)
    col = first_col + lax.broadcasted_iota(jnp.int32, (count, cols), 1)
    row = jnp.where(col < block, rank * block + col, (2 * ranks - 2 - rank) * block + col)
    return key <= row

def fwd_kernel(ranks, rank_ref, q_ref, k_ref, v_ref, o_ref, lse_ref):
    length = k_ref.shape[0]
    block = q_ref.shape[0] // 2
    rank = rank_ref[0]
    query = q_ref[...]
    value_t = v_ref[...].T
    outs, lses = [], []
    for e in range(q_ref.shape[1] // HD):
        query_e = lane_heads(query, e) * jnp.bfloat16(HD**-0.5)
        scores = []
        peak = jnp.full((1, 2 * block), negative, jnp.float32)
        for k0, k1, c0, c1, masked in segments(length, block):
            s = dot_last(k_ref[k0:k1, :], query_e[c0:c1, :])
            keep = visible(k0, k1 - k0, c0, masked, block, rank, ranks)
            if masked == c1 - c0:
                s = jnp.where(keep, s, negative)
            else:
                s = jnp.concatenate([jnp.where(keep, s[:, :masked], negative), s[:, masked:]], axis=1)
            top = jnp.max(s, axis=0, keepdims=True)
            if c0:
                top = jnp.concatenate([jnp.full((1, c0), negative, jnp.float32), top], axis=1)
            peak = jnp.maximum(peak, top)
            scores.append(s)
        total = jnp.zeros((1, 2 * block), jnp.float32)
        mixed = jnp.zeros((q_ref.shape[1], 2 * block), jnp.float32)
        for s, (k0, k1, c0, c1, masked) in zip(scores, segments(length, block)):
            w = jnp.exp(s - peak[:, c0:c1])
            part = jnp.sum(w, axis=0, keepdims=True)
            m = dot_plain(value_t[:, k0:k1], w.astype(jnp.bfloat16))
            if c0:
                part = jnp.concatenate([jnp.zeros((1, c0), jnp.float32), part], axis=1)
                m = jnp.concatenate([jnp.zeros((m.shape[0], c0), jnp.float32), m], axis=1)
            total += part
            mixed += m
        outs.append(mixed[e * HD:(e + 1) * HD] / total)
        lses.append(peak + jnp.log(total))
    o_ref[...] = jnp.concatenate(outs, axis=0).T.astype(o_ref.dtype)
    lse_ref[0] = jnp.concatenate(lses + [jnp.zeros((8 - len(lses), 2 * block), jnp.float32)], axis=0)

def attention_forward(rank, ranks, query, key, value):
    rows, width = query.shape
    length = key.shape[0]
    lanes = 2 * HD
    pairs = width // lanes
    return pl.pallas_call(
        functools.partial(fwd_kernel, ranks),
        grid=(pairs,),
        in_specs=[
            pl.BlockSpec(memory_space=pltpu.SMEM),
            pl.BlockSpec((rows, lanes), lambda i: (0, i)),
            pl.BlockSpec((length, lanes), lambda i: (0, i)),
            pl.BlockSpec((length, lanes), lambda i: (0, i)),
        ],
        out_specs=[
            pl.BlockSpec((rows, lanes), lambda i: (0, i)),
            pl.BlockSpec((1, 8, rows), lambda i: (i, 0, 0)),
        ],
        out_shape=[
            jax.ShapeDtypeStruct((rows, width), jnp.bfloat16),
            jax.ShapeDtypeStruct((pairs, 8, rows), jnp.float32),
        ],
        compiler_params=pltpu.CompilerParams(vmem_limit_bytes=48 * 2**20),
        cost_estimate=pl.CostEstimate(flops=4 * rows * length * width, bytes_accessed=4 * length * width, transcendentals=0),
        name="attention_forward",
    )(rank, query, key, value)

def bwd_kernel(ranks, step, rank_ref, q_ref, k_ref, v_ref, o_ref, g_ref, lse_ref, dq_ref, dk_ref, dv_ref):
    length = k_ref.shape[0]
    block = q_ref.shape[0] // 2
    rank = rank_ref[0]
    heads = q_ref.shape[1] // HD
    query, grad = q_ref[...], g_ref[...]
    key_t = k_ref[...].T
    spread = (grad.astype(jnp.float32) * o_ref[...].astype(jnp.float32)).T
    queries = [lane_heads(query, e) * jnp.bfloat16(HD**-0.5) for e in range(heads)]
    grads = [lane_heads(grad, e) for e in range(heads)]
    deltas = [jnp.sum(spread[e * HD:(e + 1) * HD], axis=0, keepdims=True) for e in range(heads)]
    dq = [jnp.zeros((q_ref.shape[1], 2 * block), jnp.float32) for e in range(heads)]
    for k0, k1, c0, c1, masked in segments(length, block):
        for s0 in range(k0, k1, step):
            k_c, v_c = k_ref[s0:s0 + step, :], v_ref[s0:s0 + step, :]
            keep = visible(s0, step, c0, masked, block, rank, ranks)
            dk = jnp.zeros((step, q_ref.shape[1]), jnp.float32)
            dv = jnp.zeros((step, q_ref.shape[1]), jnp.float32)
            for e in range(heads):
                s = dot_last(k_c, queries[e][c0:c1, :])
                p = jnp.exp(s - lse_ref[0, e:e + 1, c0:c1])
                if masked == c1 - c0:
                    p = jnp.where(keep, p, 0.0)
                else:
                    p = jnp.concatenate([jnp.where(keep, p[:, :masked], 0.0), p[:, masked:]], axis=1)
                dp = dot_last(v_c, grads[e][c0:c1, :])
                ds = (p * (dp - deltas[e][:, c0:c1])).astype(jnp.bfloat16)
                dv += dot_plain(p.astype(jnp.bfloat16), grads[e][c0:c1, :])
                dk += dot_plain(ds, queries[e][c0:c1, :])
                m = dot_plain(key_t[:, s0:s0 + step], ds)
                if c0:
                    m = jnp.concatenate([jnp.zeros((m.shape[0], c0), jnp.float32), m], axis=1)
                dq[e] += m
            dk_ref[s0:s0 + step, :] = dk.astype(jnp.bfloat16)
            dv_ref[s0:s0 + step, :] = dv.astype(jnp.bfloat16)
    own = jnp.concatenate([dq[e][e * HD:(e + 1) * HD] for e in range(heads)], axis=0)
    dq_ref[...] = (own * HD**-0.5).T.astype(jnp.bfloat16)

def attention_backward(rank, ranks, query, key, value, mixed, grad, lse, step=512):
    rows, width = query.shape
    length = key.shape[0]
    lanes = 2 * HD
    pairs = width // lanes
    row_spec = pl.BlockSpec((rows, lanes), lambda i: (0, i))
    key_spec = pl.BlockSpec((length, lanes), lambda i: (0, i))
    return pl.pallas_call(
        functools.partial(bwd_kernel, ranks, step),
        grid=(pairs,),
        in_specs=[
            pl.BlockSpec(memory_space=pltpu.SMEM),
            row_spec, key_spec, key_spec, row_spec, row_spec,
            pl.BlockSpec((1, 8, rows), lambda i: (i, 0, 0)),
        ],
        out_specs=[row_spec, key_spec, key_spec],
        out_shape=[
            jax.ShapeDtypeStruct((rows, width), jnp.bfloat16),
            jax.ShapeDtypeStruct((length, width), jnp.bfloat16),
            jax.ShapeDtypeStruct((length, width), jnp.bfloat16),
        ],
        compiler_params=pltpu.CompilerParams(vmem_limit_bytes=48 * 2**20),
        cost_estimate=pl.CostEstimate(flops=10 * rows * length * width, bytes_accessed=8 * length * width, transcendentals=0),
        name="attention_backward",
    )(rank, query, key, value, mixed, grad, lse)

def contract_rows(left, right):
    return lax.dot_general(
        left, right, (((0,), (0,)), ((), ())), preferred_element_type=jnp.float32
    )


def low(block):
    return block.astype(jnp.bfloat16)


def body(
    tokens,
    cotangent,
    group_ids,
    group_weights,
    gain_attn,
    w_query,
    w_latent,
    w_key,
    w_value,
    w_out,
    gain_mlp,
    w_gate,
    w_up,
    w_down,
):
    ring = Ring()
    ranks, members = ring.count, lax.axis_size("dp")
    rank, member = lax.axis_index("head"), lax.axis_index("dp")
    length, width = tokens.shape
    block = length // (2 * ranks)
    cols = w_query.shape[1]
    inner = w_key.shape[0]
    share = w_gate.shape[1] // members
    part = width // members
    order = dp_bit_order()

    def own_rows(whole, of=None):
        of = rank if of is None else of
        first = lax.dynamic_slice_in_dim(whole, of * block, block, 0)
        second = lax.dynamic_slice_in_dim(whole, (2 * ranks - 1 - of) * block, block, 0)
        return jnp.concatenate([first, second], axis=0)

    def place_rows(blocks):
        whole = jnp.zeros((length, blocks[0].shape[1]), blocks[0].dtype)
        for offset, piece in blocks.items():
            of = ring.owner(offset)
            whole = lax.dynamic_update_slice_in_dim(whole, piece[:block], of * block, 0)
            whole = lax.dynamic_update_slice_in_dim(
                whole, piece[block:], (2 * ranks - 1 - of) * block, 0
            )
        return whole

    packed = jnp.concatenate([w_query.T, w_key.T, w_value.T, w_out], axis=1)
    half_cols = cols // 2
    core = member % 2
    blocks = ring.gather(lax.dynamic_slice_in_dim(packed, core * half_cols, half_cols, 0))
    mine = jnp.zeros((ranks, half_cols, packed.shape[1]), packed.dtype)
    for offset, piece in blocks.items():
        mine = lax.dynamic_update_slice_in_dim(mine, piece[None], ring.owner(offset), 0)
    theirs = flip(mine, 1)
    first, second = jnp.where(core == 0, mine, theirs), jnp.where(core == 0, theirs, mine)
    packed = jnp.stack([first, second], axis=1).reshape(ranks * cols, packed.shape[1])
    query_t = packed[:, :width]
    key_t = packed[:, width : width + inner]
    value_t = packed[:, width + inner : width + 2 * inner]
    out_all = packed[:, width + 2 * inner :]

    gate_own = lax.dynamic_slice_in_dim(w_gate, member * share, share, 1).T
    up_own = lax.dynamic_slice_in_dim(w_up, member * share, share, 1).T
    down_own = lax.dynamic_slice_in_dim(w_down, member * share, share, 0)
    blocks = ring.gather(jnp.concatenate([gate_own, up_own, down_own], axis=0))
    offsets = list(blocks)
    gate_t = jnp.concatenate([blocks[o][:share] for o in offsets], axis=0)
    up_t = jnp.concatenate([blocks[o][share : 2 * share] for o in offsets], axis=0)
    down = jnp.concatenate([blocks[o][2 * share :] for o in offsets], axis=0)

    labels = jnp.arange(group_weights.shape[0], dtype=jnp.int32)
    row_weight = jnp.sum(jnp.where(group_ids[0] == labels, group_weights, 0.0))
    grad_out = wide(own_rows(cotangent)) * row_weight
    grad_low_all = dp_gather(low(grad_out))

    inputs = wide(tokens)
    root = lax.rsqrt(jnp.mean(inputs * inputs, axis=-1, keepdims=True) + epsilon)
    normed = low(inputs * root * gain_attn)
    latent = low(dot_plain(normed, w_latent))
    half_heads = query_t.shape[0] // 2
    latents = (latent[:, :inner], latent[:, inner:])

    def from_latents(weight_t):
        return jnp.concatenate(
            [
                low(dot_last(latents[0], weight_t[:half_heads])),
                low(dot_last(latents[1], weight_t[half_heads:])),
            ],
            axis=1,
        )

    keys, values = from_latents(key_t), from_latents(value_t)
    inputs_own, root_own, normed_own = own_rows(inputs), own_rows(root), own_rows(normed)
    queries = low(dot_last(normed_own, query_t))
    rank_ref = rank.astype(jnp.int32).reshape(1)
    mixed, lse = attention_forward(rank_ref, ranks, queries, keys, values)
    hidden = inputs_own + dot_plain(mixed, out_all)

    root_mlp = lax.rsqrt(jnp.mean(hidden * hidden, axis=-1, keepdims=True) + epsilon)
    normed_mlp = dp_gather(low(hidden * root_mlp * gain_mlp))
    gate = dot_last(normed_mlp, gate_t)
    up = dot_last(normed_mlp, up_t)
    logistic = jax.nn.sigmoid(gate)
    act = low(gate * logistic * up)
    grad_act = dot_last(grad_low_all, down)
    grad_gate = low(grad_act * up * logistic * (1.0 + gate * (1.0 - logistic)))
    grad_up = low(grad_act * gate * logistic)
    grad_normed_mlp = dp_scatter(low(dot_plain(grad_gate, gate_t) + dot_plain(grad_up, up_t)))
    mlp_out = dp_scatter(low(dot_plain(act, down)))
    block_out = place_rows(ring.gather(low(hidden + mlp_out)))

    grad_w_gate = low(contract_rows(grad_gate, normed_mlp))
    grad_w_up = low(contract_rows(grad_up, normed_mlp))
    grad_w_down = low(contract_rows(act, grad_low_all))

    def mlp_block(offset):
        spot = offsets.index(offset)
        rows = slice(spot * share, (spot + 1) * share)
        return jnp.concatenate([grad_w_gate[rows], grad_w_up[rows], grad_w_down[rows]], axis=0)

    mlp_grads = low(ring.scatter(mlp_block)).reshape(3, share, width)
    mlp_grads = wide(lax.all_to_all(mlp_grads, "dp", 2, 1, tiled=True))

    def norm_backward(incoming, gain, entered, scale):
        scaled = gain * incoming
        inner_mean = jnp.mean(scaled * entered, axis=-1, keepdims=True)
        grad = scale * scaled - entered * (scale * scale * scale) * inner_mean
        return grad, jnp.sum(incoming * entered * scale, axis=0)

    grad_hidden, grad_gain_mlp = norm_backward(grad_normed_mlp, gain_mlp, hidden, root_mlp)
    grad_hidden = grad_out + grad_hidden
    grad_hidden_low = low(grad_hidden)
    grad_mixed = low(dot_last(grad_hidden_low, out_all))

    def member_cols(whole, r):
        return lax.dynamic_slice_in_dim(whole, (member ^ order[r]) * part, part, 1)

    def by_member(left, right):
        return jnp.concatenate(
            [low(contract_rows(left, member_cols(right, r))) for r in range(members)], axis=0
        )

    grad_w_out = low(dp_scatter(by_member(mixed, grad_hidden_low)))

    grad_queries, grad_keys, grad_values = attention_backward(
        rank_ref, ranks, queries, keys, values, mixed, grad_mixed, lse
    )
    grad_latent = jnp.concatenate(
        [
            low(
                dot_plain(grad_keys[:, s], key_t[s]) + dot_plain(grad_values[:, s], value_t[s])
            )
            for s in (slice(0, half_heads), slice(half_heads, None))
        ],
        axis=1,
    )
    grad_latent_own = low(ring.scatter(lambda o: own_rows(grad_latent, ring.owner(o))))
    grad_normed = dot_plain(grad_queries, query_t) + dot_last(grad_latent_own, w_latent)
    grad_inputs, grad_gain_attn = norm_backward(grad_normed, gain_attn, inputs_own, root_own)
    grad_tokens = place_rows(ring.gather(low(grad_hidden + grad_inputs)))

    grad_w_query = by_member(grad_queries, normed_own)
    grad_w_latent = by_member(grad_latent_own, normed_own)
    rows_query = query_t.shape[0]
    rows_latent = w_latent.shape[1]
    joint = dp_scatter(
        jnp.concatenate(
            [
                grad_w_query.reshape(members, rows_query, part),
                grad_w_latent.reshape(members, rows_latent, part),
            ],
            axis=1,
        )
    )
    joint = low(joint[0])
    grad_w_kv = [
        jnp.concatenate(
            [
                low(contract_rows(latents[0], grad[:, :half_heads])),
                low(contract_rows(latents[1], grad[:, half_heads:])),
            ],
            axis=1,
        )
        for grad in (grad_keys, grad_values)
    ]
    inner_part = inner // members
    kv = low(
        dp_scatter(
            jnp.concatenate(
                [
                    lax.dynamic_slice_in_dim(g, (member ^ r) * inner_part, inner_part, 0)
                    for r in order
                    for g in grad_w_kv
                ],
                axis=0,
            )
        )
    )
    latent_cols = rows_latent // ranks

    def attn_block(offset):
        of = ring.owner(offset)
        kv_piece = lax.dynamic_slice_in_dim(kv, of * cols, cols, 1).reshape(-1, part)
        return jnp.concatenate(
            [
                lax.dynamic_slice_in_dim(grad_w_out, of * cols, cols, 0),
                lax.dynamic_slice_in_dim(joint, of * cols, cols, 0),
                lax.dynamic_slice_in_dim(joint, rows_query + of * latent_cols, latent_cols, 0),
                kv_piece,
            ],
            axis=0,
        )

    attn_grads = ring.scatter(attn_block)
    kv_grads = attn_grads[2 * cols + latent_cols :].reshape(2, inner_part, cols)

    gains = lax.psum(jnp.stack([grad_gain_attn, grad_gain_mlp]), ("head", "dp"))
    gains = lax.dynamic_slice_in_dim(gains, member * part, part, 1)
    return (
        block_out,
        grad_tokens,
        gains[0],
        attn_grads[cols : 2 * cols].T,
        attn_grads[2 * cols : 2 * cols + latent_cols].T,
        kv_grads[0],
        kv_grads[1],
        attn_grads[:cols],
        gains[1],
        mlp_grads[0].T,
        mlp_grads[1].T,
        mlp_grads[2],
    )


def solution(mesh):
    in_specs = (
        P("dp", None),
        P("dp", None),
        P("dp"),
        P(),
        P(),
        P(None, "head"),
        P(),
        P(None, "head"),
        P(None, "head"),
        P("head", None),
        P(),
        P(None, "head"),
        P(None, "head"),
        P("head", None),
    )
    out_specs = (
        P("dp", None),
        P("dp", None),
        P("dp"),
        P("dp", "head"),
        P("dp", "head"),
        P("dp", "head"),
        P("dp", "head"),
        P("head", "dp"),
        P("dp"),
        P("dp", "head"),
        P("dp", "head"),
        P("head", "dp"),
    )
    return jax.shard_map(body, mesh=mesh, in_specs=in_specs, out_specs=out_specs, check_vma=False)
```

```python
import functools

import jax
import jax.numpy as jnp
from jax import lax
from jax.experimental import pallas as pl
from jax.experimental.pallas import tpu as pltpu
from jax.sharding import PartitionSpec as P

HD = 64
epsilon = 1e-05
negative = -1e30


def snake_order(count):
    return list(range(0, count, 2)) + list(range(count - 1, 0, -2))


def after(block, *earlier):
    return lax.optimization_barrier((block, earlier))[0] if earlier else block


class Ring:
    def __init__(self):
        self.count = lax.axis_size("head")
        self.half = self.count // 2
        order = snake_order(self.count)
        self.forward = [(order[i], order[(i + 1) % self.count]) for i in range(self.count)]
        self.backward = [(b, a) for a, b in self.forward]
        index = lax.axis_index("head")
        self.place = jnp.where(index % 2 == 0, index // 2, self.count - 1 - index // 2)
        self.offsets = [0]
        for step in range(1, self.half):
            self.offsets += [-step, step]
        self.offsets.append(self.half)

    def owner(self, offset):
        spot = (self.place + offset) % self.count
        return jnp.where(spot < self.half, 2 * spot, 2 * (self.count - 1 - spot) + 1)

    def send(self, name, ahead, behind):
        with jax.named_scope(name):
            return (
                lax.ppermute(ahead, "head", self.forward),
                lax.ppermute(behind, "head", self.backward),
            )


class Gather:
    def __init__(self, name, ring, own):
        self.name, self.ring, self.blocks, self.taken = name, ring, {0: own}, 0
        self.edge = (own, own)

    def settle(self, *gates):
        *self.edge, _ = lax.optimization_barrier((*self.edge, gates))
        if 0 < self.taken < self.ring.half:
            self.blocks[-self.taken], self.blocks[self.taken] = self.edge
        elif self.taken:
            self.blocks[self.taken] = tuple(self.edge)

    def step(self, *gates):
        self.settle(*gates)
        self.taken += 1
        ahead, behind = self.given = tuple(self.edge)
        if self.taken == self.ring.half:
            cut = ahead.shape[-1] // 2
            self.edge = self.ring.send(self.name, ahead[..., :cut], behind[..., cut:])
            self.blocks[self.taken] = self.edge
        else:
            self.edge = self.ring.send(self.name, ahead, behind)
            self.blocks[-self.taken], self.blocks[self.taken] = self.edge
        return self.edge

    def last_steps(self, *gates):
        while self.taken < self.ring.half:
            self.step(*gates)
            gates = ()
        return self.blocks


class Scatter:
    def __init__(self, name, ring, block):
        self.name, self.ring, self.block, self.taken = name, ring, block, 0

    def step(self, *gates):
        left = self.ring.half - self.taken
        if self.taken == 0:
            far = after(self.block(left), *gates)
            cut = far.shape[-1] // 2
            give = far[..., :cut], far[..., cut:]
        else:
            give = self.block(left), self.block(-left)
            ahead, behind, _ = lax.optimization_barrier((*self.edge, gates))
            cut = ahead.shape[-1]
            if self.taken == 1:
                give = (
                    jnp.concatenate([add(give[0][..., :cut], ahead), give[0][..., cut:]], axis=-1),
                    jnp.concatenate([give[1][..., :cut], add(give[1][..., cut:], behind)], axis=-1),
                )
            else:
                give = add(give[0], ahead), add(give[1], behind)
        self.taken, self.given = self.taken + 1, give
        self.edge = self.ring.send(self.name, *give)
        return self.edge

    def settle(self, *gates):
        *self.edge, _ = lax.optimization_barrier((*self.edge, gates))

    def last_steps(self, *gates):
        while self.taken < self.ring.half:
            self.step(*gates)
            gates = ()
        return wide(self.block(0)) + wide(self.edge[0]) + wide(self.edge[1])


def whole_block(piece):
    return jnp.concatenate(piece, axis=-1) if isinstance(piece, tuple) else piece


def copy_kernel(plan, sources, starts_ref, *refs):
    inputs, outputs, sems = refs[:sources], refs[sources:-1], refs[-1]
    copies = []
    for i, (source, rows, cols, target, slot, target_cols) in enumerate(plan):
        count = rows[1] - rows[0]
        start = pl.multiple_of(starts_ref[slot], count)
        copies.append(
            pltpu.make_async_copy(
                inputs[source].at[rows[0] : rows[1], cols[0] : cols[1]],
                outputs[target].at[pl.ds(start, count), target_cols[0] : target_cols[1]],
                sems.at[i],
            )
        )
    for copy in copies:
        copy.start()
    for copy in copies:
        copy.wait()


def place_blocks(plan, arrays, starts, shapes):
    anywhere = pl.BlockSpec(memory_space=pl.ANY)
    moved = 2 * sum(a.size for a in arrays)
    return pl.pallas_call(
        functools.partial(copy_kernel, plan, len(arrays)),
        in_specs=[pl.BlockSpec(memory_space=pltpu.SMEM)]
        + [pl.BlockSpec(memory_space=pltpu.VMEM)] * len(arrays),
        out_specs=[anywhere] * len(shapes),
        out_shape=[jax.ShapeDtypeStruct(s, arrays[0].dtype) for s in shapes],
        scratch_shapes=[pltpu.SemaphoreType.DMA((len(plan),))],
        compiler_params=pltpu.CompilerParams(vmem_limit_bytes=40 * 2**20),
        cost_estimate=pl.CostEstimate(flops=0, bytes_accessed=2 * moved, transcendentals=0),
        name="place_blocks",
    )(jnp.stack(starts).astype(jnp.int32), *arrays)


def wide(block):
    return block.astype(jnp.float32)


def add(left, right):
    return (wide(left) + wide(right)).astype(jnp.bfloat16)


def flip(block, bit):
    count = lax.axis_size("dp")
    return lax.ppermute(block, "dp", [(i, i ^ bit) for i in range(count)])


def dp_bits():
    return lax.axis_size("dp").bit_length() - 1


def dp_gather(own, *gates):
    for bit, gate in zip(reversed(range(dp_bits())), (*gates, *[()] * dp_bits())):
        got = flip(own, 1 << bit)
        own, got, _ = lax.optimization_barrier((own, got, gate))
        own = jnp.concatenate([own, got], axis=0)
    return own


def dp_bit_order():
    order = [0]
    for bit in reversed(range(dp_bits())):
        order = order + [r | 1 << bit for r in order]
    return order


def dp_scatter_step(blocks, distance, *gates):
    half = blocks.shape[0] // 2
    return add(blocks[:half], after(flip(blocks[half:], distance), *gates))


def dp_scatter(blocks, distance=1, *gates):
    while distance < lax.axis_size("dp"):
        blocks = dp_scatter_step(blocks, distance, *gates)
        distance *= 2
    return blocks


def dp_scatter_cols(blocks):
    for bit in range(dp_bits()):
        half = blocks.shape[1] // 2
        blocks = add(blocks[:, :half], flip(blocks[:, half:], 1 << bit))
    return blocks


def dp_sum_blocks(blocks):
    distance = 1
    while distance < lax.axis_size("dp"):
        half = blocks.shape[0] // 2
        blocks = blocks[:half] + flip(blocks[half:], distance)
        distance *= 2
    return blocks


def dot_last(a, b):
    return lax.dot_general(a, b, (((1,), (1,)), ((), ())), preferred_element_type=jnp.float32)

def dot_plain(a, b):
    return jnp.dot(a, b, preferred_element_type=jnp.float32)

def lane_heads(x, e):
    lane = lax.broadcasted_iota(jnp.int32, x.shape, 1)
    return jnp.where(lane // HD == e, x, jnp.zeros_like(x))

def segments(length, block):
    half = length // 2
    if block % 128 == 0:
        return ((0, half, 0, 2 * block, block), (half, length, block, 2 * block, block))
    return ((0, half, 0, 2 * block, 2 * block), (half, length, 0, 2 * block, 2 * block))

def visible(first_key, count, first_col, cols, block, rank, ranks):
    key = first_key + lax.broadcasted_iota(jnp.int32, (count, cols), 0)
    col = first_col + lax.broadcasted_iota(jnp.int32, (count, cols), 1)
    row = jnp.where(col < block, rank * block + col, (2 * ranks - 2 - rank) * block + col)
    return key <= row

def fwd_kernel(ranks, rank_ref, q_ref, k_ref, v_ref, o_ref, lse_ref):
    length = k_ref.shape[0]
    block = q_ref.shape[0] // 2
    rank = rank_ref[0]
    query = q_ref[...]
    value_t = v_ref[...].T
    outs, lses = [], []
    for e in range(q_ref.shape[1] // HD):
        query_e = lane_heads(query, e) * jnp.bfloat16(HD**-0.5)
        scores = []
        peak = jnp.full((1, 2 * block), negative, jnp.float32)
        for k0, k1, c0, c1, masked in segments(length, block):
            s = dot_last(k_ref[k0:k1, :], query_e[c0:c1, :])
            keep = visible(k0, k1 - k0, c0, masked, block, rank, ranks)
            if masked == c1 - c0:
                s = jnp.where(keep, s, negative)
            else:
                s = jnp.concatenate([jnp.where(keep, s[:, :masked], negative), s[:, masked:]], axis=1)
            top = jnp.max(s, axis=0, keepdims=True)
            if c0:
                top = jnp.concatenate([jnp.full((1, c0), negative, jnp.float32), top], axis=1)
            peak = jnp.maximum(peak, top)
            scores.append(s)
        total = jnp.zeros((1, 2 * block), jnp.float32)
        mixed = jnp.zeros((q_ref.shape[1], 2 * block), jnp.float32)
        for s, (k0, k1, c0, c1, masked) in zip(scores, segments(length, block)):
            w = jnp.exp(s - peak[:, c0:c1])
            part = jnp.sum(w, axis=0, keepdims=True)
            m = dot_plain(value_t[:, k0:k1], w.astype(jnp.bfloat16))
            if c0:
                part = jnp.concatenate([jnp.zeros((1, c0), jnp.float32), part], axis=1)
                m = jnp.concatenate([jnp.zeros((m.shape[0], c0), jnp.float32), m], axis=1)
            total += part
            mixed += m
        outs.append(mixed[e * HD:(e + 1) * HD] / total)
        lses.append(peak + jnp.log(total))
    o_ref[...] = jnp.concatenate(outs, axis=0).T.astype(o_ref.dtype)
    lse_ref[0] = jnp.concatenate(lses + [jnp.zeros((8 - len(lses), 2 * block), jnp.float32)], axis=0)

def attention_forward(rank, ranks, query, key, value):
    rows, width = query.shape
    length = key.shape[0]
    lanes = 2 * HD
    pairs = width // lanes
    return pl.pallas_call(
        functools.partial(fwd_kernel, ranks),
        grid=(pairs,),
        in_specs=[
            pl.BlockSpec(memory_space=pltpu.SMEM),
            pl.BlockSpec((rows, lanes), lambda i: (0, i)),
            pl.BlockSpec((length, lanes), lambda i: (0, i)),
            pl.BlockSpec((length, lanes), lambda i: (0, i)),
        ],
        out_specs=[
            pl.BlockSpec((rows, lanes), lambda i: (0, i)),
            pl.BlockSpec((1, 8, rows), lambda i: (i, 0, 0)),
        ],
        out_shape=[
            jax.ShapeDtypeStruct((rows, width), jnp.bfloat16),
            jax.ShapeDtypeStruct((pairs, 8, rows), jnp.float32),
        ],
        compiler_params=pltpu.CompilerParams(vmem_limit_bytes=48 * 2**20),
        cost_estimate=pl.CostEstimate(flops=4 * rows * length * width, bytes_accessed=4 * length * width, transcendentals=0),
        name="attention_forward",
    )(rank, query, key, value)

def bwd_kernel(ranks, step, rank_ref, q_ref, k_ref, v_ref, o_ref, g_ref, lse_ref, dq_ref, dk_ref, dv_ref):
    length = k_ref.shape[0]
    block = q_ref.shape[0] // 2
    rank = rank_ref[0]
    heads = q_ref.shape[1] // HD
    query, grad = q_ref[...], g_ref[...]
    key_t = k_ref[...].T
    spread = (grad.astype(jnp.float32) * o_ref[...].astype(jnp.float32)).T
    queries = [lane_heads(query, e) * jnp.bfloat16(HD**-0.5) for e in range(heads)]
    grads = [lane_heads(grad, e) for e in range(heads)]
    deltas = [jnp.sum(spread[e * HD:(e + 1) * HD], axis=0, keepdims=True) for e in range(heads)]
    dq = [jnp.zeros((q_ref.shape[1], 2 * block), jnp.float32) for e in range(heads)]
    for k0, k1, c0, c1, masked in segments(length, block):
        for s0 in range(k0, k1, step):
            k_c, v_c = k_ref[s0:s0 + step, :], v_ref[s0:s0 + step, :]
            keep = visible(s0, step, c0, masked, block, rank, ranks)
            dk = jnp.zeros((step, q_ref.shape[1]), jnp.float32)
            dv = jnp.zeros((step, q_ref.shape[1]), jnp.float32)
            for e in range(heads):
                s = dot_last(k_c, queries[e][c0:c1, :])
                p = jnp.exp(s - lse_ref[0, e:e + 1, c0:c1])
                if masked == c1 - c0:
                    p = jnp.where(keep, p, 0.0)
                else:
                    p = jnp.concatenate([jnp.where(keep, p[:, :masked], 0.0), p[:, masked:]], axis=1)
                dp = dot_last(v_c, grads[e][c0:c1, :])
                ds = (p * (dp - deltas[e][:, c0:c1])).astype(jnp.bfloat16)
                dv += dot_plain(p.astype(jnp.bfloat16), grads[e][c0:c1, :])
                dk += dot_plain(ds, queries[e][c0:c1, :])
                m = dot_plain(key_t[:, s0:s0 + step], ds)
                if c0:
                    m = jnp.concatenate([jnp.zeros((m.shape[0], c0), jnp.float32), m], axis=1)
                dq[e] += m
            dk_ref[s0:s0 + step, :] = dk.astype(jnp.bfloat16)
            dv_ref[s0:s0 + step, :] = dv.astype(jnp.bfloat16)
    own = jnp.concatenate([dq[e][e * HD:(e + 1) * HD] for e in range(heads)], axis=0)
    dq_ref[...] = (own * HD**-0.5).T.astype(jnp.bfloat16)

def attention_backward(rank, ranks, query, key, value, mixed, grad, lse, step=512):
    rows, width = query.shape
    length = key.shape[0]
    lanes = 2 * HD
    pairs = width // lanes
    row_spec = pl.BlockSpec((rows, lanes), lambda i: (0, i))
    key_spec = pl.BlockSpec((length, lanes), lambda i: (0, i))
    return pl.pallas_call(
        functools.partial(bwd_kernel, ranks, step),
        grid=(pairs,),
        in_specs=[
            pl.BlockSpec(memory_space=pltpu.SMEM),
            row_spec, key_spec, key_spec, row_spec, row_spec,
            pl.BlockSpec((1, 8, rows), lambda i: (i, 0, 0)),
        ],
        out_specs=[row_spec, key_spec, key_spec],
        out_shape=[
            jax.ShapeDtypeStruct((rows, width), jnp.bfloat16),
            jax.ShapeDtypeStruct((length, width), jnp.bfloat16),
            jax.ShapeDtypeStruct((length, width), jnp.bfloat16),
        ],
        compiler_params=pltpu.CompilerParams(vmem_limit_bytes=48 * 2**20),
        cost_estimate=pl.CostEstimate(flops=10 * rows * length * width, bytes_accessed=8 * length * width, transcendentals=0),
        name="attention_backward",
    )(rank, query, key, value, mixed, grad, lse)

def contract_rows(left, right):
    return lax.dot_general(
        left, right, (((0,), (0,)), ((), ())), preferred_element_type=jnp.float32
    )


def low(block):
    return block.astype(jnp.bfloat16)


def body(
    tokens,
    cotangent,
    group_ids,
    group_weights,
    gain_attn,
    w_query,
    w_latent,
    w_key,
    w_value,
    w_out,
    gain_mlp,
    w_gate,
    w_up,
    w_down,
):
    ring = Ring()
    ranks, members = ring.count, lax.axis_size("dp")
    rank, member = lax.axis_index("head"), lax.axis_index("dp")
    length, width = tokens.shape
    block = length // (2 * ranks)
    cols = w_query.shape[1]
    inner = w_key.shape[0]
    share = w_gate.shape[1] // members
    part = width // members
    order = dp_bit_order()
    offsets = ring.offsets

    def own_rows(whole, of=None):
        of = rank if of is None else of
        first = lax.dynamic_slice_in_dim(whole, of * block, block, 0)
        second = lax.dynamic_slice_in_dim(whole, (2 * ranks - 1 - of) * block, block, 0)
        return jnp.concatenate([first, second], axis=0)

    def place_rows(blocks):
        plan, arrays, starts = [], [], []
        for offset, piece in blocks.items():
            of = ring.owner(offset)
            first = 0
            for array in piece if isinstance(piece, tuple) else (piece,):
                last = first + array.shape[1]
                for slot in range(2):
                    plan.append(
                        (
                            len(arrays),
                            (slot * block, (slot + 1) * block),
                            (0, array.shape[1]),
                            0,
                            len(starts) + slot,
                            (first, last),
                        )
                    )
                arrays.append(array)
                first = last
            starts += [of * block, (2 * ranks - 1 - of) * block]
        return place_blocks(plan, arrays, starts, [(length, width)])[0]

    def member_cols(whole):
        return jnp.concatenate(
            [lax.dynamic_slice_in_dim(whole, (member ^ r) * part, part, 1) for r in order], axis=1
        )

    core = member % 2
    packed = jnp.concatenate([w_query.T, w_key.T, w_value.T, w_out], axis=1)
    half_cols = cols // 2
    attn_ring = Gather("attn_weights", ring, lax.dynamic_slice_in_dim(packed, core * half_cols, half_cols, 0))
    a1 = attn_ring.step()
    inputs = wide(tokens)
    root = lax.rsqrt(jnp.mean(inputs * inputs, axis=-1, keepdims=True) + epsilon)
    normed = low(inputs * root * gain_attn)
    a2 = attn_ring.step(normed)
    latent = low(dot_plain(after(normed, *a1), w_latent))

    labels = jnp.arange(group_weights.shape[0], dtype=jnp.int32)
    row_weight = jnp.sum(jnp.where(group_ids[0] == labels, group_weights, 0.0))
    grad_out = wide(own_rows(after(cotangent, *a1))) * row_weight
    grad_low = low(grad_out)
    a3 = attn_ring.step(latent)

    gate_w, up_w, down_w, *_ = lax.optimization_barrier((w_gate, w_up, w_down, *a2))
    units = jnp.concatenate(
        [
            lax.dynamic_slice_in_dim(gate_w, member * share, share, 1).T,
            lax.dynamic_slice_in_dim(up_w, member * share, share, 1).T,
            lax.dynamic_slice_in_dim(down_w, member * share, share, 0),
        ],
        axis=1,
    )
    attn_ring.step(units, grad_low)
    unit_ring = Gather("mlp_weights", ring, units)
    w1 = unit_ring.step(*a3)

    blocks = attn_ring.last_steps()
    mine = jnp.stack([whole_block(blocks[o]) for o in offsets]).reshape(-1, packed.shape[1])
    theirs = flip(mine, 1)
    edges = (0, width, width + inner, width + 2 * inner, 2 * width + 2 * inner)
    plan, starts = [], []
    for spot, offset in enumerate(offsets):
        for source in range(2):
            for target in range(4):
                plan.append(
                    (
                        source,
                        (spot * half_cols, (spot + 1) * half_cols),
                        (edges[target], edges[target + 1]),
                        target,
                        len(starts),
                        (0, edges[target + 1] - edges[target]),
                    )
                )
            starts.append(ring.owner(offset) * cols + (core ^ source) * half_cols)
    query_t, key_t, value_t, out_all = place_blocks(
        plan,
        [mine, theirs],
        starts,
        [(ranks * cols, edges[t + 1] - edges[t]) for t in range(4)],
    )

    inputs_own = wide(own_rows(after(tokens, *a2)))
    root_own = lax.rsqrt(jnp.mean(inputs_own * inputs_own, axis=-1, keepdims=True) + epsilon)
    normed_own = low(inputs_own * root_own * gain_attn)
    rank_ref = rank.astype(jnp.int32).reshape(1)
    groups = [
        (slice(j * width // 2, (j + 1) * width // 2), latent[:, j * inner : (j + 1) * inner])
        for j in range(2)
    ]
    kept, mixed = [], ()
    for s, latent_j in groups:
        latent_j, normed_j, _ = lax.optimization_barrier((latent_j, normed_own, mixed))
        keys = low(dot_last(latent_j, key_t[s]))
        values = low(dot_last(latent_j, value_t[s]))
        queries = low(dot_last(normed_j, query_t[s]))
        if not kept:
            queries = after(queries, *w1)
            w2 = unit_ring.step()
        mixed, lse = attention_forward(rank_ref, ranks, queries, keys, values)
        kept.append((queries, keys, values, mixed, lse))
    w3 = unit_ring.step(mixed)
    grad_low_all = dp_gather(grad_low, kept[0][3], kept[1][3])
    hidden = inputs_own + dot_plain(kept[0][3], out_all[groups[0][0]])
    hidden += dot_plain(kept[1][3], out_all[groups[1][0]])

    root_mlp = lax.rsqrt(jnp.mean(hidden * hidden, axis=-1, keepdims=True) + epsilon)
    normed_mlp = dp_gather(low(hidden * root_mlp * gain_mlp), w3)
    blocks = unit_ring.last_steps()
    units = jnp.concatenate([whole_block(blocks[o]) for o in offsets], axis=0)
    gate_t, up_t, down = units[:, :width], units[:, width : 2 * width], units[:, 2 * width :]
    gate = dot_last(normed_mlp, gate_t)
    up = dot_last(normed_mlp, up_t)
    logistic = jax.nn.sigmoid(gate)
    act = low(gate * logistic * up)
    grad_act = dot_last(grad_low_all, down)
    grad_gate = low(grad_act * up * logistic * (1.0 + gate * (1.0 - logistic)))
    grad_up = low(grad_act * gate * logistic)
    normed_part = low(dot_plain(grad_gate, gate_t) + dot_plain(grad_up, up_t))
    normed_sum = dp_scatter_step(normed_part, 1)
    mlp_sum = dp_scatter_step(after(low(dot_plain(act, down)), normed_sum), 1)
    grad_gate, grad_up, act, *_ = lax.optimization_barrier((grad_gate, grad_up, act, mlp_sum))
    grad_units = jnp.concatenate(
        [
            low(contract_rows(grad_gate, normed_mlp)),
            low(contract_rows(grad_up, normed_mlp)),
            low(contract_rows(act, grad_low_all)),
        ],
        axis=1,
    )

    def unit_rows(offset):
        spot = offsets.index(offset)
        return grad_units[spot * share : (spot + 1) * share]

    unit_sums = Scatter("mlp_grads", ring, unit_rows)
    r1 = unit_sums.step()

    def norm_backward(incoming, gain, entered, scale):
        scaled = gain * incoming
        inner_mean = jnp.mean(scaled * entered, axis=-1, keepdims=True)
        grad = scale * scaled - entered * (scale * scale * scale) * inner_mean
        return grad, jnp.sum(incoming * entered * scale, axis=0)

    incoming = wide(dp_scatter(normed_sum, 2, grad_units))
    grad_hidden, grad_gain_mlp = norm_backward(incoming, gain_mlp, hidden, root_mlp)
    grad_hidden = grad_out + grad_hidden
    grad_hidden_low = low(grad_hidden)
    r2 = unit_sums.step(grad_hidden_low)
    mlp_out = dp_scatter(after(mlp_sum, grad_hidden_low), 2)

    grads = []
    grad_hidden_late = after(grad_hidden_low, *r1)
    before = ()
    for (s, latent_j), (queries, keys, values, mixed, lse) in zip(groups, kept):
        grad_mixed = after(low(dot_last(grad_hidden_late, out_all[s])), *before)
        grads.append(
            attention_backward(rank_ref, ranks, queries, keys, values, mixed, grad_mixed, lse)
        )
        if len(grads) == 1:
            before = (*r2, grads[0][0])
            r3 = unit_sums.step(grads[0][0], mlp_out)
    r4 = unit_sums.step(r2, grads[1][0])
    grads, _ = lax.optimization_barrier((grads, unit_sums.given))
    grad_latent = [
        low(dot_plain(g[1], key_t[s]) + dot_plain(g[2], value_t[s]))
        for (s, _), g in zip(groups, grads)
    ]
    grad_latent = jnp.concatenate(grad_latent, axis=1)
    latent_sums = Scatter("latent_grads", ring, lambda o: own_rows(grad_latent, ring.owner(o)))
    block_ring = Gather("block_out", ring, low(hidden + mlp_out))
    edge = (*r4, *latent_sums.step())
    hidden_late = after(grad_hidden_low, latent_sums.given)
    for _ in range(ring.half - 1):
        edge = (*latent_sums.step(*edge), *block_ring.step(*edge))
    block_ring.last_steps(*edge)
    grad_latent_own = low(latent_sums.last_steps())
    grad_normed = dot_last(grad_latent_own, w_latent)
    for (s, _), g in zip(groups, grads):
        grad_normed += dot_plain(g[0], query_t[s])
    grad_inputs, grad_gain_attn = norm_backward(grad_normed, gain_attn, inputs_own, root_own)
    gain_rows = jnp.stack([low(grad_gain_attn), low(grad_gain_mlp)])
    gain_rows = jnp.concatenate([gain_rows, jnp.zeros((14, width), jnp.bfloat16)], axis=0)
    token_ring = Gather(
        "grad_tokens",
        ring,
        jnp.concatenate([low(grad_hidden + grad_inputs), gain_rows], axis=0),
    )
    edge = (*token_ring.step(), *block_ring.edge)
    unit_sums.settle(token_ring.given)
    mlp_grads = low(unit_sums.last_steps()).reshape(share, 3, width)
    mlp_grads = wide(lax.all_to_all(mlp_grads, "dp", 2, 0, tiled=True))
    block_out = place_rows(block_ring.blocks)

    hidden_cols = member_cols(hidden_late)
    normed_cols = member_cols(normed_own)
    grad_w_out = dp_scatter_cols(
        jnp.concatenate([low(contract_rows(k[3], hidden_cols)) for k in kept], axis=0)
    )
    lefts = (grads[0][0], grads[1][0], grad_latent_own)
    joint = dp_scatter_cols(
        jnp.concatenate([low(contract_rows(left, normed_cols)) for left in lefts], axis=0)
    )
    inner_part = inner // members
    grad_w_kv = [
        jnp.concatenate(
            [low(contract_rows(latent_j, g[i])) for (_, latent_j), g in zip(groups, grads)],
            axis=1,
        )
        for i in (1, 2)
    ]
    kv = low(
        dp_scatter(
            jnp.concatenate(
                [
                    lax.dynamic_slice_in_dim(g, (member ^ r) * inner_part, inner_part, 0)
                    for r in order
                    for g in grad_w_kv
                ],
                axis=0,
            )
        )
    )
    grad_w_out, joint = low(grad_w_out), low(joint)
    latent_cols = w_latent.shape[1] // ranks
    side_by_side = 2 * cols == part

    def attn_block(offset):
        of = ring.owner(offset)
        kv_piece = lax.dynamic_slice_in_dim(kv, of * cols, cols, 1)
        if side_by_side:
            kv_piece = jnp.concatenate([kv_piece[:inner_part], kv_piece[inner_part:]], axis=1)
        return jnp.concatenate(
            [
                lax.dynamic_slice_in_dim(grad_w_out, of * cols, cols, 0),
                lax.dynamic_slice_in_dim(joint, of * cols, cols, 0),
                lax.dynamic_slice_in_dim(joint, ranks * cols + of * latent_cols, latent_cols, 0),
                kv_piece.reshape(-1, part),
            ],
            axis=0,
        )

    attn_sums = Scatter("attn_grads", ring, attn_block)
    for step in range(ring.half - 1):
        edge = (*token_ring.step(*edge), *attn_sums.step(*edge))
        if step == 0:
            edge = (*edge, block_out)
    attn_grads = attn_sums.last_steps(*edge)
    kv_grads = attn_grads[2 * cols + latent_cols :]
    if side_by_side:
        kv_grads = kv_grads[:, :cols], kv_grads[:, cols:]
    else:
        kv_grads = kv_grads.reshape(2, inner_part, cols)
    grad_tokens = place_rows(token_ring.last_steps())

    gains = sum(
        wide(whole_block(piece)[2 * block : 2 * block + 2]) for piece in token_ring.blocks.values()
    )
    gains = jnp.stack(
        [lax.dynamic_slice_in_dim(gains, (member ^ r) * part, part, 1) for r in order]
    )
    gains = dp_sum_blocks(gains)[0]
    return (
        block_out,
        grad_tokens,
        gains[0],
        attn_grads[cols : 2 * cols].T,
        attn_grads[2 * cols : 2 * cols + latent_cols].T,
        kv_grads[0],
        kv_grads[1],
        attn_grads[:cols],
        gains[1],
        mlp_grads[:, 0].T,
        mlp_grads[:, 1].T,
        mlp_grads[:, 2],
    )


def solution(mesh):
    in_specs = (
        P("dp", None),
        P("dp", None),
        P("dp"),
        P(),
        P(),
        P(None, "head"),
        P(),
        P(None, "head"),
        P(None, "head"),
        P("head", None),
        P(),
        P(None, "head"),
        P(None, "head"),
        P("head", None),
    )
    out_specs = (
        P("dp", None),
        P("dp", None),
        P("dp"),
        P("dp", "head"),
        P("dp", "head"),
        P("dp", "head"),
        P("dp", "head"),
        P("head", "dp"),
        P("dp"),
        P("dp", "head"),
        P("dp", "head"),
        P("head", "dp"),
    )
    return jax.shard_map(body, mesh=mesh, in_specs=in_specs, out_specs=out_specs, check_vma=False)
```

```python
import functools

import jax
import jax.numpy as jnp
from jax import lax
from jax.experimental import pallas as pl
from jax.experimental.pallas import tpu as pltpu
from jax.sharding import PartitionSpec as P

HD = 64
epsilon = 1e-05
negative = -1e30


def snake_order(count):
    return list(range(0, count, 2)) + list(range(count - 1, 0, -2))


def after(block, *earlier):
    return lax.optimization_barrier((block, earlier))[0] if earlier else block


class Ring:
    def __init__(self):
        self.count = lax.axis_size("head")
        self.half = self.count // 2
        order = snake_order(self.count)
        self.forward = [(order[i], order[(i + 1) % self.count]) for i in range(self.count)]
        self.backward = [(b, a) for a, b in self.forward]
        index = lax.axis_index("head")
        self.place = jnp.where(index % 2 == 0, index // 2, self.count - 1 - index // 2)
        self.offsets = [0]
        for step in range(1, self.half):
            self.offsets += [-step, step]
        self.offsets.append(self.half)

    def owner(self, offset):
        spot = (self.place + offset) % self.count
        return jnp.where(spot < self.half, 2 * spot, 2 * (self.count - 1 - spot) + 1)

    def send(self, name, ahead, behind):
        with jax.named_scope(name):
            return (
                lax.ppermute(ahead, "head", self.forward),
                lax.ppermute(behind, "head", self.backward),
            )


class Gather:
    def __init__(self, name, ring, own):
        self.name, self.ring, self.blocks, self.taken = name, ring, {0: own}, 0
        self.edge = (own, own)

    def settle(self, *gates):
        *self.edge, _ = lax.optimization_barrier((*self.edge, gates))
        if 0 < self.taken < self.ring.half:
            self.blocks[-self.taken], self.blocks[self.taken] = self.edge
        elif self.taken:
            self.blocks[self.taken] = tuple(self.edge)
        return self.edge

    def step(self, *gates):
        self.settle(*gates)
        self.taken += 1
        ahead, behind = self.given = tuple(self.edge)
        if self.taken == self.ring.half:
            cut = ahead.shape[-1] // 2
            self.edge = self.ring.send(self.name, ahead[..., :cut], behind[..., cut:])
            self.blocks[self.taken] = self.edge
        else:
            self.edge = self.ring.send(self.name, ahead, behind)
            self.blocks[-self.taken], self.blocks[self.taken] = self.edge
        return self.edge

    def last_steps(self, *gates):
        while self.taken < self.ring.half:
            self.step(*gates)
            gates = ()
        return self.blocks


class Scatter:
    def __init__(self, name, ring, block):
        self.name, self.ring, self.block, self.taken = name, ring, block, 0

    def step(self, *gates):
        left = self.ring.half - self.taken
        if self.taken == 0:
            far = after(self.block(left), *gates)
            cut = far.shape[-1] // 2
            give = far[..., :cut], far[..., cut:]
        else:
            give = self.block(left), self.block(-left)
            ahead, behind, _ = lax.optimization_barrier((*self.edge, gates))
            cut = ahead.shape[-1]
            if self.taken == 1:
                give = (
                    jnp.concatenate([add(give[0][..., :cut], ahead), give[0][..., cut:]], axis=-1),
                    jnp.concatenate([give[1][..., :cut], add(give[1][..., cut:], behind)], axis=-1),
                )
            else:
                give = add(give[0], ahead), add(give[1], behind)
        self.taken, self.given = self.taken + 1, give
        self.edge = self.ring.send(self.name, *give)
        return self.edge

    def settle(self, *gates):
        *self.edge, _ = lax.optimization_barrier((*self.edge, gates))
        return self.edge

    def last_steps(self, *gates):
        while self.taken < self.ring.half:
            self.step(*gates)
            gates = ()
        return wide(self.block(0)) + wide(self.edge[0]) + wide(self.edge[1])


def whole_block(piece):
    return jnp.concatenate(piece, axis=-1) if isinstance(piece, tuple) else piece


def copy_kernel(plan, sources, starts_ref, *refs):
    inputs, outputs, sems = refs[:sources], refs[sources:-1], refs[-1]
    copies = []
    for i, (source, rows, cols, target, slot, target_cols) in enumerate(plan):
        count = rows[1] - rows[0]
        start = pl.multiple_of(starts_ref[slot], count)
        copies.append(
            pltpu.make_async_copy(
                inputs[source].at[rows[0] : rows[1], cols[0] : cols[1]],
                outputs[target].at[pl.ds(start, count), target_cols[0] : target_cols[1]],
                sems.at[i],
            )
        )
    for copy in copies:
        copy.start()
    for copy in copies:
        copy.wait()


def place_blocks(plan, arrays, starts, shapes):
    anywhere = pl.BlockSpec(memory_space=pl.ANY)
    return pl.pallas_call(
        functools.partial(copy_kernel, plan, len(arrays)),
        in_specs=[pl.BlockSpec(memory_space=pltpu.SMEM)]
        + [pl.BlockSpec(memory_space=pltpu.VMEM)] * len(arrays),
        out_specs=[anywhere] * len(shapes),
        out_shape=[jax.ShapeDtypeStruct(s, arrays[0].dtype) for s in shapes],
        scratch_shapes=[pltpu.SemaphoreType.DMA((len(plan),))],
        compiler_params=pltpu.CompilerParams(vmem_limit_bytes=20 * 2**20),
        cost_estimate=pl.CostEstimate(flops=0, bytes_accessed=0, transcendentals=0),
        name="place_blocks",
    )(jnp.stack(starts).astype(jnp.int32), *arrays)


def wide(block):
    return block.astype(jnp.float32)


def add(left, right):
    return (wide(left) + wide(right)).astype(jnp.bfloat16)


def flip(block, bit):
    count = lax.axis_size("dp")
    return lax.ppermute(block, "dp", [(i, i ^ bit) for i in range(count)])


def dp_bits():
    return lax.axis_size("dp").bit_length() - 1


def dp_gather(own, *gates):
    for bit, gate in zip(reversed(range(dp_bits())), (*gates, *[()] * dp_bits())):
        got = flip(own, 1 << bit)
        own, got, _ = lax.optimization_barrier((own, got, gate))
        own = jnp.concatenate([own, got], axis=0)
    return own


def dp_gather_rest(own):
    for bit in reversed(range(dp_bits() - 1)):
        own = jnp.concatenate([own, flip(own, 1 << bit)], axis=0)
    return own


def dp_bit_order():
    order = [0]
    for bit in reversed(range(dp_bits())):
        order = order + [r | 1 << bit for r in order]
    return order


def dp_scatter_step(blocks, distance, *gates):
    half = blocks.shape[0] // 2
    return add(blocks[:half], after(flip(blocks[half:], distance), *gates))


def dp_scatter(blocks, distance=1, *gates):
    while distance < lax.axis_size("dp"):
        blocks = dp_scatter_step(blocks, distance, *gates)
        distance *= 2
    return blocks


def dp_scatter_cols_step(blocks, distance):
    half = blocks.shape[1] // 2
    return add(blocks[:, :half], flip(blocks[:, half:], distance))


def dp_scatter_cols(blocks, distance=1):
    while distance < lax.axis_size("dp"):
        blocks = dp_scatter_cols_step(blocks, distance)
        distance *= 2
    return blocks


def dp_sum_blocks(blocks):
    distance = 1
    while distance < lax.axis_size("dp"):
        half = blocks.shape[0] // 2
        blocks = blocks[:half] + flip(blocks[half:], distance)
        distance *= 2
    return blocks


def dot_last(a, b):
    return lax.dot_general(a, b, (((1,), (1,)), ((), ())), preferred_element_type=jnp.float32)

def dot_plain(a, b):
    return jnp.dot(a, b, preferred_element_type=jnp.float32)

def lane_heads(x, e):
    lane = lax.broadcasted_iota(jnp.int32, x.shape, 1)
    return jnp.where(lane // HD == e, x, jnp.zeros_like(x))

def segments(length, block):
    half = length // 2
    if block % 128 == 0:
        return ((0, half, 0, 2 * block, block), (half, length, block, 2 * block, block))
    return ((0, half, 0, 2 * block, 2 * block), (half, length, 0, 2 * block, 2 * block))

def visible(first_key, count, first_col, cols, block, rank, ranks):
    key = first_key + lax.broadcasted_iota(jnp.int32, (count, cols), 0)
    col = first_col + lax.broadcasted_iota(jnp.int32, (count, cols), 1)
    row = jnp.where(col < block, rank * block + col, (ranks - 1 + rank) * block + col)
    return key <= row

def fwd_heads(ranks, rank_ref, q_ref, k_ref, v_ref, o_ref, lse_ref):
    length = k_ref.shape[0]
    block = q_ref.shape[0] // 2
    rank = rank_ref[0]
    query = q_ref[...]
    value_t = v_ref[...].T
    outs, lses = [], []
    for e in range(q_ref.shape[1] // HD):
        query_e = lane_heads(query, e) * jnp.bfloat16(HD**-0.5)
        scores = []
        peak = jnp.full((1, 2 * block), negative, jnp.float32)
        for k0, k1, c0, c1, masked in segments(length, block):
            s = dot_last(k_ref[k0:k1, :], query_e[c0:c1, :])
            keep = visible(k0, k1 - k0, c0, masked, block, rank, ranks)
            if masked == c1 - c0:
                s = jnp.where(keep, s, negative)
            else:
                s = jnp.concatenate([jnp.where(keep, s[:, :masked], negative), s[:, masked:]], axis=1)
            top = jnp.max(s, axis=0, keepdims=True)
            if c0:
                top = jnp.concatenate([jnp.full((1, c0), negative, jnp.float32), top], axis=1)
            peak = jnp.maximum(peak, top)
            scores.append(s)
        total = jnp.zeros((1, 2 * block), jnp.float32)
        mixed = jnp.zeros((q_ref.shape[1], 2 * block), jnp.float32)
        for s, (k0, k1, c0, c1, masked) in zip(scores, segments(length, block)):
            w = jnp.exp(s - peak[:, c0:c1])
            part = jnp.sum(w, axis=0, keepdims=True)
            m = dot_plain(value_t[:, k0:k1], w.astype(jnp.bfloat16))
            if c0:
                part = jnp.concatenate([jnp.zeros((1, c0), jnp.float32), part], axis=1)
                m = jnp.concatenate([jnp.zeros((m.shape[0], c0), jnp.float32), m], axis=1)
            total += part
            mixed += m
        outs.append(mixed[e * HD:(e + 1) * HD] / total)
        lses.append(peak + jnp.log(total))
    o_ref[...] = jnp.concatenate(outs, axis=0).T.astype(o_ref.dtype)
    lse_ref[0] = jnp.concatenate(lses + [jnp.zeros((8 - len(lses), 2 * block), jnp.float32)], axis=0)

def fwd_kernel(ranks, split, rank_ref, q_ref, *refs):
    keys, values, outs = refs[:2], refs[2:4], refs[4:]
    for j in range(2):

        @pl.when(pl.program_id(0) // split == j)
        def _():
            fwd_heads(ranks, rank_ref, q_ref, keys[j], values[j], *outs)


def attention_forward(rank, ranks, query, keys, values):
    rows, width = query.shape
    length = keys[0].shape[0]
    lanes = 2 * HD
    pairs = width // lanes
    split = pairs // 2
    key_specs = [
        pl.BlockSpec((length, lanes), lambda i: (0, jnp.minimum(i, split - 1))),
        pl.BlockSpec((length, lanes), lambda i: (0, jnp.maximum(i - split, 0))),
    ]
    return pl.pallas_call(
        functools.partial(fwd_kernel, ranks, split),
        grid=(pairs,),
        in_specs=[
            pl.BlockSpec(memory_space=pltpu.SMEM),
            pl.BlockSpec((rows, lanes), lambda i: (0, i)),
            *key_specs,
            *key_specs,
        ],
        out_specs=[
            pl.BlockSpec((rows, lanes), lambda i: (0, i)),
            pl.BlockSpec((1, 8, rows), lambda i: (i, 0, 0)),
        ],
        out_shape=[
            jax.ShapeDtypeStruct((rows, width), jnp.bfloat16),
            jax.ShapeDtypeStruct((pairs, 8, rows), jnp.float32),
        ],
        compiler_params=pltpu.CompilerParams(vmem_limit_bytes=20 * 2**20),
        cost_estimate=pl.CostEstimate(flops=0, bytes_accessed=0, transcendentals=0),
        name="attention_forward",
    )(rank, query, *keys, *values)


def bwd_kernel(ranks, step, rank_ref, q_ref, k_ref, v_ref, o_ref, g_ref, lse_ref, dq_ref, dk_ref, dv_ref):
    length = k_ref.shape[0]
    block = q_ref.shape[0] // 2
    rank = rank_ref[0]
    heads = q_ref.shape[1] // HD
    query, grad = q_ref[...], g_ref[...]
    key_t = k_ref[...].T
    spread = (grad.astype(jnp.float32) * o_ref[...].astype(jnp.float32)).T
    queries = [lane_heads(query, e) * jnp.bfloat16(HD**-0.5) for e in range(heads)]
    grads = [lane_heads(grad, e) for e in range(heads)]
    deltas = [jnp.sum(spread[e * HD:(e + 1) * HD], axis=0, keepdims=True) for e in range(heads)]
    dq = [jnp.zeros((q_ref.shape[1], 2 * block), jnp.float32) for e in range(heads)]
    for k0, k1, c0, c1, masked in segments(length, block):
        for s0 in range(k0, k1, step):
            k_c, v_c = k_ref[s0:s0 + step, :], v_ref[s0:s0 + step, :]
            keep = visible(s0, step, c0, masked, block, rank, ranks)
            dk = jnp.zeros((step, q_ref.shape[1]), jnp.float32)
            dv = jnp.zeros((step, q_ref.shape[1]), jnp.float32)
            for e in range(heads):
                s = dot_last(k_c, queries[e][c0:c1, :])
                p = jnp.exp(s - lse_ref[0, e:e + 1, c0:c1])
                if masked == c1 - c0:
                    p = jnp.where(keep, p, 0.0)
                else:
                    p = jnp.concatenate([jnp.where(keep, p[:, :masked], 0.0), p[:, masked:]], axis=1)
                dp = dot_last(v_c, grads[e][c0:c1, :])
                ds = (p * (dp - deltas[e][:, c0:c1])).astype(jnp.bfloat16)
                dv += dot_plain(p.astype(jnp.bfloat16), grads[e][c0:c1, :])
                dk += dot_plain(ds, queries[e][c0:c1, :])
                m = dot_plain(key_t[:, s0:s0 + step], ds)
                if c0:
                    m = jnp.concatenate([jnp.zeros((m.shape[0], c0), jnp.float32), m], axis=1)
                dq[e] += m
            dk_ref[s0:s0 + step, :] = dk.astype(jnp.bfloat16)
            dv_ref[s0:s0 + step, :] = dv.astype(jnp.bfloat16)
    own = jnp.concatenate([dq[e][e * HD:(e + 1) * HD] for e in range(heads)], axis=0)
    dq_ref[...] = (own * HD**-0.5).T.astype(jnp.bfloat16)

def attention_backward(rank, ranks, first, query, key, value, mixed, grad, lse, step=512):
    rows = query.shape[0]
    length, width = key.shape
    lanes = 2 * HD
    pairs = width // lanes
    row_spec = pl.BlockSpec((rows, lanes), lambda i: (0, i + first))
    key_spec = pl.BlockSpec((length, lanes), lambda i: (0, i))
    return pl.pallas_call(
        functools.partial(bwd_kernel, ranks, step),
        grid=(pairs,),
        in_specs=[
            pl.BlockSpec(memory_space=pltpu.SMEM),
            row_spec, key_spec, key_spec, row_spec, row_spec,
            pl.BlockSpec((1, 8, rows), lambda i: (i + first, 0, 0)),
        ],
        out_specs=[pl.BlockSpec((rows, lanes), lambda i: (0, i)), key_spec, key_spec],
        out_shape=[
            jax.ShapeDtypeStruct((rows, width), jnp.bfloat16),
            jax.ShapeDtypeStruct((length, width), jnp.bfloat16),
            jax.ShapeDtypeStruct((length, width), jnp.bfloat16),
        ],
        compiler_params=pltpu.CompilerParams(vmem_limit_bytes=20 * 2**20),
        cost_estimate=pl.CostEstimate(flops=0, bytes_accessed=0, transcendentals=0),
        name="attention_backward",
    )(rank, query, key, value, mixed, grad, lse)

def contract_rows(left, right):
    return lax.dot_general(
        left, right, (((0,), (0,)), ((), ())), preferred_element_type=jnp.float32
    )


def low(block):
    return block.astype(jnp.bfloat16)


def body(
    tokens,
    cotangent,
    group_ids,
    group_weights,
    gain_attn,
    w_query,
    w_latent,
    w_key,
    w_value,
    w_out,
    gain_mlp,
    w_gate,
    w_up,
    w_down,
):
    ring = Ring()
    ranks, members = ring.count, lax.axis_size("dp")
    rank, member = lax.axis_index("head"), lax.axis_index("dp")
    length, width = tokens.shape
    block = length // (2 * ranks)
    cols = w_query.shape[1]
    inner = w_key.shape[0]
    share = w_gate.shape[1] // members
    part = width // members
    order = dp_bit_order()
    offsets = ring.offsets

    def own_rows(whole, of=None):
        of = rank if of is None else of
        first = lax.dynamic_slice_in_dim(whole, of * block, block, 0)
        second = lax.dynamic_slice_in_dim(whole, (ranks + of) * block, block, 0)
        return jnp.concatenate([first, second], axis=0)

    def place_rows(blocks):
        plan, arrays, starts = [], [], []
        for offset, piece in blocks.items():
            of = ring.owner(offset)
            first = 0
            for array in piece if isinstance(piece, tuple) else (piece,):
                last = first + array.shape[1]
                for slot in range(2):
                    plan.append(
                        (
                            len(arrays),
                            (slot * block, (slot + 1) * block),
                            (0, array.shape[1]),
                            0,
                            len(starts) + slot,
                            (first, last),
                        )
                    )
                arrays.append(array)
                first = last
            starts += [of * block, (ranks + of) * block]
        return place_blocks(plan, arrays, starts, [(length, width)])[0]

    def member_cols(whole):
        return jnp.concatenate(
            [lax.dynamic_slice_in_dim(whole, (member ^ r) * part, part, 1) for r in order], axis=1
        )

    core = member % 2
    packed = jnp.concatenate([w_query.T, w_key.T, w_value.T, w_out], axis=1)
    half_cols = cols // 2
    attn_ring = Gather("attn_weights", ring, lax.dynamic_slice_in_dim(packed, core * half_cols, half_cols, 0))
    a1 = attn_ring.step()
    inputs = wide(tokens)
    root = lax.rsqrt(jnp.mean(inputs * inputs, axis=-1, keepdims=True) + epsilon)
    normed = low(inputs * root * gain_attn)
    a2 = attn_ring.step(normed)
    labels = jnp.arange(group_weights.shape[0], dtype=jnp.int32)
    row_weight = jnp.sum(jnp.where(group_ids[0] == labels, group_weights, 0.0))
    grad_out = wide(own_rows(cotangent)) * row_weight
    grad_low = low(grad_out)
    grad_low_pair = flip(grad_low, members // 2)
    latent = low(dot_plain(after(normed, *a1), w_latent))

    grad_low_pair, latent, _ = lax.optimization_barrier((grad_low_pair, latent, attn_ring.settle(latent)))
    a3 = attn_ring.step(grad_low_pair)
    grad_low_all = dp_gather_rest(jnp.concatenate([grad_low, grad_low_pair], axis=0))

    gate_w, up_w, down_w, *_ = lax.optimization_barrier((w_gate, w_up, w_down, *a2))
    units = jnp.concatenate(
        [
            lax.dynamic_slice_in_dim(gate_w, member * share, share, 1).T,
            lax.dynamic_slice_in_dim(up_w, member * share, share, 1).T,
            lax.dynamic_slice_in_dim(down_w, member * share, share, 0),
        ],
        axis=1,
    )
    attn_ring.step(units, grad_low_all)
    unit_ring = Gather("mlp_weights", ring, units)
    w1 = unit_ring.step(*a3)

    blocks = attn_ring.last_steps()
    mine = jnp.stack([whole_block(blocks[o]) for o in offsets]).reshape(-1, packed.shape[1])
    theirs = flip(mine, 1)
    edges = (0, width, width + inner, width + 2 * inner, 2 * width + 2 * inner)
    plan, starts = [], []
    for spot, offset in enumerate(offsets):
        for source in range(2):
            for target in range(4):
                plan.append(
                    (
                        source,
                        (spot * half_cols, (spot + 1) * half_cols),
                        (edges[target], edges[target + 1]),
                        target,
                        len(starts),
                        (0, edges[target + 1] - edges[target]),
                    )
                )
            starts.append(ring.owner(offset) * cols + (core ^ source) * half_cols)
    query_t, key_t, value_t, out_all = place_blocks(
        plan,
        [mine, theirs],
        starts,
        [(ranks * cols, edges[t + 1] - edges[t]) for t in range(4)],
    )

    inputs_own = wide(own_rows(after(tokens, theirs)))
    root_own = lax.rsqrt(jnp.mean(inputs_own * inputs_own, axis=-1, keepdims=True) + epsilon)
    normed_own = low(inputs_own * root_own * gain_attn)
    rank_ref = rank.astype(jnp.int32).reshape(1)
    groups = [
        (slice(j * width // 2, (j + 1) * width // 2), latent[:, j * inner : (j + 1) * inner])
        for j in range(2)
    ]
    queries = low(dot_last(normed_own, query_t))
    keys = [low(dot_last(latent_j, key_t[s])) for s, latent_j in groups]
    values = [low(dot_last(latent_j, value_t[s])) for s, latent_j in groups]
    queries, w1 = lax.optimization_barrier((queries, unit_ring.settle(queries, keys, values)))
    w2 = unit_ring.step()
    mixed, lse = attention_forward(rank_ref, ranks, queries, keys, values)
    w2 = unit_ring.settle(mixed)
    w3 = unit_ring.step()
    hidden = inputs_own + dot_plain(mixed, out_all)

    root_mlp = lax.rsqrt(jnp.mean(hidden * hidden, axis=-1, keepdims=True) + epsilon)
    normed_mlp = low(hidden * root_mlp * gain_mlp)
    unit_ring.settle(normed_mlp)
    normed_pair = flip(normed_mlp, members // 2)
    unit_ring.last_steps(normed_pair)
    blocks, _ = lax.optimization_barrier((unit_ring.blocks, normed_mlp))
    normed_mlp = dp_gather_rest(jnp.concatenate([normed_mlp, normed_pair], axis=0))
    units = jnp.concatenate([whole_block(blocks[o]) for o in offsets], axis=0)
    gate_t, up_t, down = units[:, :width], units[:, width : 2 * width], units[:, 2 * width :]
    gate = dot_last(normed_mlp, gate_t)
    up = dot_last(normed_mlp, up_t)
    logistic = jax.nn.sigmoid(gate)
    act = low(gate * logistic * up)
    grad_act = dot_last(grad_low_all, down)
    grad_gate = low(grad_act * up * logistic * (1.0 + gate * (1.0 - logistic)))
    grad_up = low(grad_act * gate * logistic)
    normed_part = low(dot_plain(grad_gate, gate_t) + dot_plain(grad_up, up_t))
    normed_sum = dp_scatter_step(normed_part, 1)
    mlp_sum = dp_scatter_step(after(low(dot_plain(act, down)), normed_sum), 1)
    grad_gate, grad_up, act, *_ = lax.optimization_barrier((grad_gate, grad_up, act, mlp_sum))
    grad_units = jnp.concatenate(
        [
            low(contract_rows(grad_gate, normed_mlp)),
            low(contract_rows(grad_up, normed_mlp)),
            low(contract_rows(act, grad_low_all)),
        ],
        axis=1,
    )

    def unit_rows(offset):
        spot = offsets.index(offset)
        return grad_units[spot * share : (spot + 1) * share]

    unit_sums = Scatter("mlp_grads", ring, unit_rows)
    r1 = unit_sums.step()

    def norm_backward(incoming, gain, entered, scale):
        scaled = gain * incoming
        inner_mean = jnp.mean(scaled * entered, axis=-1, keepdims=True)
        grad = scale * scaled - entered * (scale * scale * scale) * inner_mean
        return grad, jnp.sum(incoming * entered * scale, axis=0)

    incoming = wide(dp_scatter(normed_sum, 2, grad_units))
    grad_hidden, grad_gain_mlp = norm_backward(incoming, gain_mlp, hidden, root_mlp)
    grad_hidden = grad_out + grad_hidden
    grad_hidden_low = low(grad_hidden)
    r2 = unit_sums.step(grad_hidden_low)
    mlp_out = dp_scatter(after(mlp_sum, grad_hidden_low), 2)

    grad_mixed = low(dot_last(after(grad_hidden_low, *r1), out_all))
    pairs = width // (4 * HD)
    grads = [
        attention_backward(rank_ref, ranks, 0, queries, keys[0], values[0], mixed, grad_mixed, lse)
    ]
    r2 = unit_sums.settle(grads[0][0], mlp_out)
    grad_mixed, block_own, _ = lax.optimization_barrier((grad_mixed, low(hidden + mlp_out), r2))
    r3 = unit_sums.step()
    block_ring = Gather("block_out", ring, block_own)
    b1 = block_ring.step()
    grads.append(
        attention_backward(
            rank_ref, ranks, pairs, queries, keys[1], values[1], mixed, grad_mixed, lse
        )
    )
    r4 = unit_sums.step(grads[1][0], b1)
    grads, _ = lax.optimization_barrier((grads, unit_sums.given))
    grad_latent = [
        low(dot_plain(g[1], key_t[s]) + dot_plain(g[2], value_t[s]))
        for (s, _), g in zip(groups, grads)
    ]
    grad_latent = jnp.concatenate(grad_latent, axis=1)
    latent_sums = Scatter("latent_grads", ring, lambda o: own_rows(grad_latent, ring.owner(o)))
    edge = (*r4, *latent_sums.step())

    hidden_late, grads_late, _ = lax.optimization_barrier(
        (grad_hidden_low, grads, latent_sums.given)
    )
    hidden_cols = member_cols(hidden_late)
    grad_w_out = dp_scatter_cols_step(low(contract_rows(mixed, hidden_cols)), 1)
    inner_part = inner // members
    grad_w_kv = [
        jnp.concatenate(
            [low(contract_rows(latent_j, g[i])) for (_, latent_j), g in zip(groups, grads_late)],
            axis=1,
        )
        for i in (1, 2)
    ]
    kv = jnp.concatenate(
        [
            lax.dynamic_slice_in_dim(g, (member ^ r) * inner_part, inner_part, 0)
            for r in order
            for g in grad_w_kv
        ],
        axis=0,
    )
    kv = dp_scatter_step(kv, 1)
    normed_cols = member_cols(normed_own)
    grad_w_query = jnp.concatenate([g[0] for g in grads_late], axis=1)
    grad_w_query = low(contract_rows(grad_w_query, normed_cols))
    for step in range(ring.half - 1):
        if step == 1:
            edge = (edge, grad_w_out, kv)
            grad_w_out, kv = dp_scatter_cols(grad_w_out, 2), dp_scatter(kv, 2)
            grad_w_query = dp_scatter_cols_step(grad_w_query, 1)
        if step == 2:
            edge = (edge, grad_w_out, kv, grad_w_query)
            grad_w_query = dp_scatter_cols(grad_w_query, 2)
        edge = (*latent_sums.step(*edge), *block_ring.step(*edge))
    block_ring.last_steps()
    grad_latent_own = low(latent_sums.last_steps())
    grad_normed = dot_last(grad_latent_own, w_latent)
    for (s, _), g in zip(groups, grads):
        grad_normed += dot_plain(g[0], query_t[s])
    grad_inputs, grad_gain_attn = norm_backward(grad_normed, gain_attn, inputs_own, root_own)
    gain_rows = jnp.stack([low(grad_gain_attn), low(grad_gain_mlp)])
    gain_rows = jnp.concatenate([gain_rows, jnp.zeros((14, width), jnp.bfloat16)], axis=0)
    token_ring = Gather(
        "grad_tokens",
        ring,
        jnp.concatenate([low(grad_hidden + grad_inputs), gain_rows], axis=0),
    )
    edge = token_ring.step(*block_ring.edge)
    unit_sums.settle(*edge)
    mlp_grads = low(unit_sums.last_steps())
    mlp_grads = jnp.concatenate(
        [
            jnp.concatenate(
                [mlp_grads[:, w * width + m * part : w * width + (m + 1) * part] for w in range(3)],
                axis=1,
            )
            for m in range(members)
        ],
        axis=0,
    )
    grad_w_latent = low(contract_rows(grad_latent_own, normed_cols))
    grad_w_latent = dp_scatter_cols(grad_w_latent)
    latent_cols = w_latent.shape[1] // ranks
    side_by_side = 2 * cols == part

    def attn_block(offset):
        of = ring.owner(offset)
        kv_piece = lax.dynamic_slice_in_dim(kv, of * cols, cols, 1)
        if side_by_side:
            kv_piece = jnp.concatenate([kv_piece[:inner_part], kv_piece[inner_part:]], axis=1)
        return jnp.concatenate(
            [
                lax.dynamic_slice_in_dim(grad_w_out, of * cols, cols, 0),
                lax.dynamic_slice_in_dim(grad_w_query, of * cols, cols, 0),
                lax.dynamic_slice_in_dim(grad_w_latent, of * latent_cols, latent_cols, 0),
                kv_piece.reshape(-1, part),
            ],
            axis=0,
        )

    attn_sums = Scatter("attn_grads", ring, attn_block)
    for step in range(ring.half - 1):
        edge = (*token_ring.step(*edge), *attn_sums.step(*edge))
        if step == 0:
            mlp_grads = lax.all_to_all(after(mlp_grads, edge), "dp", 0, 0, tiled=True)
        if step == 1:
            mlp_grads, blocks, _ = lax.optimization_barrier((mlp_grads, block_ring.blocks, edge))
            mlp_grads, block_out = wide(mlp_grads), place_rows(blocks)
    attn_grads = attn_sums.last_steps(*edge)
    kv_grads = attn_grads[2 * cols + latent_cols :]
    if side_by_side:
        kv_grads = kv_grads[:, :cols], kv_grads[:, cols:]
    else:
        kv_grads = kv_grads.reshape(2, inner_part, cols)
    grad_tokens = place_rows(token_ring.last_steps())

    gains = sum(
        wide(whole_block(piece)[2 * block : 2 * block + 2]) for piece in token_ring.blocks.values()
    )
    gains = jnp.stack(
        [lax.dynamic_slice_in_dim(gains, (member ^ r) * part, part, 1) for r in order]
    )
    gains = dp_sum_blocks(gains)[0]
    return (
        block_out,
        grad_tokens,
        gains[0],
        attn_grads[cols : 2 * cols].T,
        attn_grads[2 * cols : 2 * cols + latent_cols].T,
        kv_grads[0],
        kv_grads[1],
        attn_grads[:cols],
        gains[1],
        mlp_grads[:, :part].T,
        mlp_grads[:, part : 2 * part].T,
        mlp_grads[:, 2 * part :],
    )


def solution(mesh):
    in_specs = (
        P("dp", None),
        P("dp", None),
        P("dp"),
        P(),
        P(),
        P(None, "head"),
        P(),
        P(None, "head"),
        P(None, "head"),
        P("head", None),
        P(),
        P(None, "head"),
        P(None, "head"),
        P("head", None),
    )
    out_specs = (
        P("dp", None),
        P("dp", None),
        P("dp"),
        P("dp", "head"),
        P("dp", "head"),
        P("dp", "head"),
        P("dp", "head"),
        P("head", "dp"),
        P("dp"),
        P("dp", "head"),
        P("dp", "head"),
        P("head", "dp"),
    )
    return jax.shard_map(body, mesh=mesh, in_specs=in_specs, out_specs=out_specs, check_vma=False)
```

```python
import functools

import jax
import jax.numpy as jnp
from jax import lax
from jax.experimental import pallas as pl
from jax.experimental.pallas import tpu as pltpu
from jax.sharding import PartitionSpec as P

HD = 64
epsilon = 1e-05
negative = -1e30


def snake_order(count):
    return list(range(0, count, 2)) + list(range(count - 1, 0, -2))


def after(block, *earlier):
    return lax.optimization_barrier((block, earlier))[0] if earlier else block


class Ring:
    def __init__(self):
        self.count = lax.axis_size("head")
        self.half = self.count // 2
        order = snake_order(self.count)
        self.forward = [(order[i], order[(i + 1) % self.count]) for i in range(self.count)]
        self.backward = [(b, a) for a, b in self.forward]
        index = lax.axis_index("head")
        self.place = jnp.where(index % 2 == 0, index // 2, self.count - 1 - index // 2)
        self.offsets = [0]
        for step in range(1, self.half):
            self.offsets += [-step, step]
        self.offsets.append(self.half)

    def owner(self, offset):
        spot = (self.place + offset) % self.count
        return jnp.where(spot < self.half, 2 * spot, 2 * (self.count - 1 - spot) + 1)

    def send(self, name, ahead, behind):
        with jax.named_scope(name):
            return (
                lax.ppermute(ahead, "head", self.forward),
                lax.ppermute(behind, "head", self.backward),
            )


class Gather:
    def __init__(self, name, ring, own):
        self.name, self.ring, self.blocks, self.taken = name, ring, {0: own}, 0
        self.edge = (own, own)

    def settle(self, *gates):
        *self.edge, _ = lax.optimization_barrier((*self.edge, gates))
        if 0 < self.taken < self.ring.half:
            self.blocks[-self.taken], self.blocks[self.taken] = self.edge
        elif self.taken:
            self.blocks[self.taken] = tuple(self.edge)
        return self.edge

    def step(self, *gates):
        self.settle(*gates)
        self.taken += 1
        ahead, behind = self.given = tuple(self.edge)
        if self.taken == self.ring.half:
            cut = ahead.shape[-1] // 2
            self.edge = self.ring.send(self.name, ahead[..., :cut], behind[..., cut:])
            self.blocks[self.taken] = self.edge
        else:
            self.edge = self.ring.send(self.name, ahead, behind)
            self.blocks[-self.taken], self.blocks[self.taken] = self.edge
        return self.edge

    def last_steps(self, *gates):
        while self.taken < self.ring.half:
            self.step(*gates)
            gates = ()
        return self.blocks


class Scatter:
    def __init__(self, name, ring, block):
        self.name, self.ring, self.block, self.taken = name, ring, block, 0

    def step(self, *gates):
        left = self.ring.half - self.taken
        if self.taken == 0:
            far = after(self.block(left), *gates)
            cut = far.shape[-1] // 2
            give = far[..., :cut], far[..., cut:]
        else:
            give = self.block(left), self.block(-left)
            ahead, behind, _ = lax.optimization_barrier((*self.edge, gates))
            cut = ahead.shape[-1]
            if self.taken == 1:
                give = (
                    jnp.concatenate([add(give[0][..., :cut], ahead), give[0][..., cut:]], axis=-1),
                    jnp.concatenate([give[1][..., :cut], add(give[1][..., cut:], behind)], axis=-1),
                )
            else:
                give = add(give[0], ahead), add(give[1], behind)
        self.taken, self.given = self.taken + 1, give
        self.edge = self.ring.send(self.name, *give)
        return self.edge

    def settle(self, *gates):
        *self.edge, _ = lax.optimization_barrier((*self.edge, gates))
        return self.edge

    def last_steps(self, *gates):
        while self.taken < self.ring.half:
            self.step(*gates)
            gates = ()
        return wide(self.block(0)) + wide(self.edge[0]) + wide(self.edge[1])


def whole_block(piece):
    return jnp.concatenate(piece, axis=-1) if isinstance(piece, tuple) else piece


def stack_blocks(blocks, offsets):
    return jnp.concatenate([whole_block(blocks[o]) for o in offsets], axis=0)


def copy_kernel(plan, sources, starts_ref, *refs):
    inputs, outputs, sems = refs[:sources], refs[sources:-1], refs[-1]
    copies = []
    for i, (source, rows, cols, target, slot, target_cols) in enumerate(plan):
        count = rows[1] - rows[0]
        start = pl.multiple_of(starts_ref[slot], count)
        copies.append(
            pltpu.make_async_copy(
                inputs[source].at[rows[0] : rows[1], cols[0] : cols[1]],
                outputs[target].at[pl.ds(start, count), target_cols[0] : target_cols[1]],
                sems.at[i],
            )
        )
    for copy in copies:
        copy.start()
    for copy in copies:
        copy.wait()


def place_blocks(plan, arrays, starts, shapes):
    anywhere = pl.BlockSpec(memory_space=pl.ANY)
    return pl.pallas_call(
        functools.partial(copy_kernel, plan, len(arrays)),
        in_specs=[pl.BlockSpec(memory_space=pltpu.SMEM)]
        + [pl.BlockSpec(memory_space=pltpu.VMEM)] * len(arrays),
        out_specs=[anywhere] * len(shapes),
        out_shape=[jax.ShapeDtypeStruct(s, arrays[0].dtype) for s in shapes],
        scratch_shapes=[pltpu.SemaphoreType.DMA((len(plan),))],
        compiler_params=pltpu.CompilerParams(vmem_limit_bytes=20 * 2**20),
        cost_estimate=pl.CostEstimate(flops=0, bytes_accessed=0, transcendentals=0),
        name="place_blocks",
    )(jnp.stack(starts).astype(jnp.int32), *arrays)


def wide(block):
    return block.astype(jnp.float32)


def add(left, right):
    return (wide(left) + wide(right)).astype(jnp.bfloat16)


def flip(block, bit):
    count = lax.axis_size("dp")
    return lax.ppermute(block, "dp", [(i, i ^ bit) for i in range(count)])


def dp_bits():
    return lax.axis_size("dp").bit_length() - 1


def dp_gather(own, *gates):
    for bit, gate in zip(reversed(range(dp_bits())), (*gates, *[()] * dp_bits())):
        got = flip(own, 1 << bit)
        own, got, _ = lax.optimization_barrier((own, got, gate))
        own = jnp.concatenate([own, got], axis=0)
    return own


def dp_gather_rest(own):
    for bit in reversed(range(dp_bits() - 1)):
        own = jnp.concatenate([own, flip(own, 1 << bit)], axis=0)
    return own


def dp_bit_order():
    order = [0]
    for bit in reversed(range(dp_bits())):
        order = order + [r | 1 << bit for r in order]
    return order


def dp_scatter_step(blocks, distance, *gates):
    half = blocks.shape[0] // 2
    return add(blocks[:half], after(flip(blocks[half:], distance), *gates))


def dp_scatter(blocks, distance=1, *gates):
    while distance < lax.axis_size("dp"):
        blocks = dp_scatter_step(blocks, distance, *gates)
        distance *= 2
    return blocks


def dp_scatter_cols_step(blocks, distance):
    half = blocks.shape[1] // 2
    return add(blocks[:, :half], flip(blocks[:, half:], distance))


def dp_scatter_cols(blocks, distance=1):
    while distance < lax.axis_size("dp"):
        blocks = dp_scatter_cols_step(blocks, distance)
        distance *= 2
    return blocks


def dp_sum_blocks(blocks):
    distance = 1
    while distance < lax.axis_size("dp"):
        half = blocks.shape[0] // 2
        blocks = blocks[:half] + flip(blocks[half:], distance)
        distance *= 2
    return blocks


def dot_last(a, b):
    return lax.dot_general(a, b, (((1,), (1,)), ((), ())), preferred_element_type=jnp.float32)

def dot_plain(a, b):
    return jnp.dot(a, b, preferred_element_type=jnp.float32)

def lane_heads(x, e):
    lane = lax.broadcasted_iota(jnp.int32, x.shape, 1)
    return jnp.where(lane // HD == e, x, jnp.zeros_like(x))

def segments(length, block):
    half = length // 2
    if block % 128 == 0:
        return ((0, half, 0, 2 * block, block), (half, length, block, 2 * block, block))
    return ((0, half, 0, 2 * block, 2 * block), (half, length, 0, 2 * block, 2 * block))

def visible(first_key, count, first_col, cols, block, rank, ranks):
    key = first_key + lax.broadcasted_iota(jnp.int32, (count, cols), 0)
    col = first_col + lax.broadcasted_iota(jnp.int32, (count, cols), 1)
    row = jnp.where(col < block, rank * block + col, (ranks - 1 + rank) * block + col)
    return key <= row

def fwd_heads(ranks, rank_ref, q_ref, k_ref, v_ref, o_ref, lse_ref):
    length = k_ref.shape[0]
    block = q_ref.shape[0] // 2
    rank = rank_ref[0]
    query = q_ref[...]
    value_t = v_ref[...].T
    outs, lses = [], []
    for e in range(q_ref.shape[1] // HD):
        query_e = lane_heads(query, e) * jnp.bfloat16(HD**-0.5)
        scores = []
        peak = jnp.full((1, 2 * block), negative, jnp.float32)
        for k0, k1, c0, c1, masked in segments(length, block):
            s = dot_last(k_ref[k0:k1, :], query_e[c0:c1, :])
            keep = visible(k0, k1 - k0, c0, masked, block, rank, ranks)
            if masked == c1 - c0:
                s = jnp.where(keep, s, negative)
            else:
                s = jnp.concatenate([jnp.where(keep, s[:, :masked], negative), s[:, masked:]], axis=1)
            top = jnp.max(s, axis=0, keepdims=True)
            if c0:
                top = jnp.concatenate([jnp.full((1, c0), negative, jnp.float32), top], axis=1)
            peak = jnp.maximum(peak, top)
            scores.append(s)
        total = jnp.zeros((1, 2 * block), jnp.float32)
        mixed = jnp.zeros((q_ref.shape[1], 2 * block), jnp.float32)
        for s, (k0, k1, c0, c1, masked) in zip(scores, segments(length, block)):
            w = jnp.exp(s - peak[:, c0:c1])
            part = jnp.sum(w, axis=0, keepdims=True)
            m = dot_plain(value_t[:, k0:k1], w.astype(jnp.bfloat16))
            if c0:
                part = jnp.concatenate([jnp.zeros((1, c0), jnp.float32), part], axis=1)
                m = jnp.concatenate([jnp.zeros((m.shape[0], c0), jnp.float32), m], axis=1)
            total += part
            mixed += m
        outs.append(mixed[e * HD:(e + 1) * HD] / total)
        lses.append(peak + jnp.log(total))
    o_ref[...] = jnp.concatenate(outs, axis=0).T.astype(o_ref.dtype)
    lse_ref[0] = jnp.concatenate(lses + [jnp.zeros((8 - len(lses), 2 * block), jnp.float32)], axis=0)

def fwd_kernel(ranks, split, rank_ref, q_ref, *refs):
    keys, values, outs = refs[:2], refs[2:4], refs[4:]
    for j in range(2):

        @pl.when(pl.program_id(0) // split == j)
        def _():
            fwd_heads(ranks, rank_ref, q_ref, keys[j], values[j], *outs)


def attention_forward(rank, ranks, query, keys, values):
    rows, width = query.shape
    length = keys[0].shape[0]
    lanes = 2 * HD
    pairs = width // lanes
    split = pairs // 2
    key_specs = [
        pl.BlockSpec((length, lanes), lambda i: (0, jnp.minimum(i, split - 1))),
        pl.BlockSpec((length, lanes), lambda i: (0, jnp.maximum(i - split, 0))),
    ]
    return pl.pallas_call(
        functools.partial(fwd_kernel, ranks, split),
        grid=(pairs,),
        in_specs=[
            pl.BlockSpec(memory_space=pltpu.SMEM),
            pl.BlockSpec((rows, lanes), lambda i: (0, i)),
            *key_specs,
            *key_specs,
        ],
        out_specs=[
            pl.BlockSpec((rows, lanes), lambda i: (0, i)),
            pl.BlockSpec((1, 8, rows), lambda i: (i, 0, 0)),
        ],
        out_shape=[
            jax.ShapeDtypeStruct((rows, width), jnp.bfloat16),
            jax.ShapeDtypeStruct((pairs, 8, rows), jnp.float32),
        ],
        compiler_params=pltpu.CompilerParams(vmem_limit_bytes=20 * 2**20),
        cost_estimate=pl.CostEstimate(flops=0, bytes_accessed=0, transcendentals=0),
        name="attention_forward",
    )(rank, query, *keys, *values)


def bwd_kernel(ranks, step, rank_ref, q_ref, k_ref, v_ref, o_ref, g_ref, lse_ref, dq_ref, dk_ref, dv_ref):
    length = k_ref.shape[0]
    block = q_ref.shape[0] // 2
    rank = rank_ref[0]
    heads = q_ref.shape[1] // HD
    query, grad = q_ref[...], g_ref[...]
    key_t = k_ref[...].T
    spread = (grad.astype(jnp.float32) * o_ref[...].astype(jnp.float32)).T
    queries = [lane_heads(query, e) * jnp.bfloat16(HD**-0.5) for e in range(heads)]
    grads = [lane_heads(grad, e) for e in range(heads)]
    deltas = [jnp.sum(spread[e * HD:(e + 1) * HD], axis=0, keepdims=True) for e in range(heads)]
    dq = [jnp.zeros((q_ref.shape[1], 2 * block), jnp.float32) for e in range(heads)]
    for k0, k1, c0, c1, masked in segments(length, block):
        for s0 in range(k0, k1, step):
            k_c, v_c = k_ref[s0:s0 + step, :], v_ref[s0:s0 + step, :]
            keep = visible(s0, step, c0, masked, block, rank, ranks)
            dk = jnp.zeros((step, q_ref.shape[1]), jnp.float32)
            dv = jnp.zeros((step, q_ref.shape[1]), jnp.float32)
            for e in range(heads):
                s = dot_last(k_c, queries[e][c0:c1, :])
                p = jnp.exp(s - lse_ref[0, e:e + 1, c0:c1])
                if masked == c1 - c0:
                    p = jnp.where(keep, p, 0.0)
                else:
                    p = jnp.concatenate([jnp.where(keep, p[:, :masked], 0.0), p[:, masked:]], axis=1)
                dp = dot_last(v_c, grads[e][c0:c1, :])
                ds = (p * (dp - deltas[e][:, c0:c1])).astype(jnp.bfloat16)
                dv += dot_plain(p.astype(jnp.bfloat16), grads[e][c0:c1, :])
                dk += dot_plain(ds, queries[e][c0:c1, :])
                m = dot_plain(key_t[:, s0:s0 + step], ds)
                if c0:
                    m = jnp.concatenate([jnp.zeros((m.shape[0], c0), jnp.float32), m], axis=1)
                dq[e] += m
            dk_ref[s0:s0 + step, :] = dk.astype(jnp.bfloat16)
            dv_ref[s0:s0 + step, :] = dv.astype(jnp.bfloat16)
    own = jnp.concatenate([dq[e][e * HD:(e + 1) * HD] for e in range(heads)], axis=0)
    dq_ref[...] = (own * HD**-0.5).T.astype(jnp.bfloat16)

def attention_backward(rank, ranks, first, query, key, value, mixed, grad, lse, step=512):
    rows = query.shape[0]
    length, width = key.shape
    lanes = 2 * HD
    pairs = width // lanes
    row_spec = pl.BlockSpec((rows, lanes), lambda i: (0, i + first))
    key_spec = pl.BlockSpec((length, lanes), lambda i: (0, i))
    return pl.pallas_call(
        functools.partial(bwd_kernel, ranks, step),
        grid=(pairs,),
        in_specs=[
            pl.BlockSpec(memory_space=pltpu.SMEM),
            row_spec, key_spec, key_spec, row_spec, row_spec,
            pl.BlockSpec((1, 8, rows), lambda i: (i + first, 0, 0)),
        ],
        out_specs=[pl.BlockSpec((rows, lanes), lambda i: (0, i)), key_spec, key_spec],
        out_shape=[
            jax.ShapeDtypeStruct((rows, width), jnp.bfloat16),
            jax.ShapeDtypeStruct((length, width), jnp.bfloat16),
            jax.ShapeDtypeStruct((length, width), jnp.bfloat16),
        ],
        compiler_params=pltpu.CompilerParams(vmem_limit_bytes=20 * 2**20),
        cost_estimate=pl.CostEstimate(flops=0, bytes_accessed=0, transcendentals=0),
        name="attention_backward",
    )(rank, query, key, value, mixed, grad, lse)

def contract_rows(left, right):
    return lax.dot_general(
        left, right, (((0,), (0,)), ((), ())), preferred_element_type=jnp.float32
    )


def low(block):
    return block.astype(jnp.bfloat16)


def body(
    tokens,
    cotangent,
    group_ids,
    group_weights,
    gain_attn,
    w_query,
    w_latent,
    w_key,
    w_value,
    w_out,
    gain_mlp,
    w_gate,
    w_up,
    w_down,
):
    ring = Ring()
    ranks, members = ring.count, lax.axis_size("dp")
    rank, member = lax.axis_index("head"), lax.axis_index("dp")
    length, width = tokens.shape
    block = length // (2 * ranks)
    cols = w_query.shape[1]
    inner = w_key.shape[0]
    share = w_gate.shape[1] // members
    part = width // members
    order = dp_bit_order()
    offsets = ring.offsets

    def own_rows(whole, of=None):
        of = rank if of is None else of
        first = lax.dynamic_slice_in_dim(whole, of * block, block, 0)
        second = lax.dynamic_slice_in_dim(whole, (ranks + of) * block, block, 0)
        return jnp.concatenate([first, second], axis=0)

    def place_rows(blocks):
        plan, arrays, starts = [], [], []
        for offset, piece in blocks.items():
            of = ring.owner(offset)
            first = 0
            for array in piece if isinstance(piece, tuple) else (piece,):
                last = first + array.shape[1]
                for slot in range(2):
                    plan.append(
                        (
                            len(arrays),
                            (slot * block, (slot + 1) * block),
                            (0, array.shape[1]),
                            0,
                            len(starts) + slot,
                            (first, last),
                        )
                    )
                arrays.append(array)
                first = last
            starts += [of * block, (ranks + of) * block]
        return place_blocks(plan, arrays, starts, [(length, width)])[0]

    def member_cols(whole):
        return jnp.concatenate(
            [lax.dynamic_slice_in_dim(whole, (member ^ r) * part, part, 1) for r in order], axis=1
        )

    core = member % 2
    packed = jnp.concatenate([w_query.T, w_key.T, w_value.T, w_out], axis=1)
    half_cols = cols // 2
    attn_ring = Gather("attn_weights", ring, lax.dynamic_slice_in_dim(packed, core * half_cols, half_cols, 0))
    a1 = attn_ring.step()
    inputs = wide(tokens)
    root = lax.rsqrt(jnp.mean(inputs * inputs, axis=-1, keepdims=True) + epsilon)
    normed = low(inputs * root * gain_attn)
    a2 = attn_ring.step(normed)
    labels = jnp.arange(group_weights.shape[0], dtype=jnp.int32)
    row_weight = jnp.sum(jnp.where(group_ids[0] == labels, group_weights, 0.0))
    grad_out = wide(own_rows(cotangent)) * row_weight
    grad_low = low(grad_out)
    grad_low_pair = flip(grad_low, members // 2)
    latent = low(dot_plain(after(normed, *a1), w_latent))

    grad_low_pair, latent, _ = lax.optimization_barrier((grad_low_pair, latent, attn_ring.settle(latent)))
    a3 = attn_ring.step(grad_low_pair)
    grad_low_all = dp_gather_rest(jnp.concatenate([grad_low, grad_low_pair], axis=0))

    gate_w, up_w, down_w, *_ = lax.optimization_barrier((w_gate, w_up, w_down, *a2))
    units = jnp.concatenate(
        [
            lax.dynamic_slice_in_dim(gate_w, member * share, share, 1).T,
            lax.dynamic_slice_in_dim(up_w, member * share, share, 1).T,
            lax.dynamic_slice_in_dim(down_w, member * share, share, 0),
        ],
        axis=1,
    )
    early = [0, -1, 1, -2, 2] if ring.half > 3 else [0]
    mine = [stack_blocks(attn_ring.blocks, early)]
    theirs = [flip(mine[0], 1)]
    attn_ring.step(units, grad_low_all, theirs[0])
    unit_ring = Gather("mlp_weights", ring, units)
    w1 = unit_ring.step(*a3)

    blocks = attn_ring.last_steps()
    late = [o for o in offsets if o not in early]
    mine.append(stack_blocks(blocks, late))
    theirs.append(flip(mine[1], 1))
    edges = (0, width, width + inner, width + 2 * inner, 2 * width + 2 * inner)
    plan, starts = [], []
    for spot, offset in enumerate(early + late):
        bundle = int(spot >= len(early))
        row = (spot - bundle * len(early)) * half_cols
        for source in range(2):
            for target in range(4):
                plan.append(
                    (
                        2 * bundle + source,
                        (row, row + half_cols),
                        (edges[target], edges[target + 1]),
                        target,
                        len(starts),
                        (0, edges[target + 1] - edges[target]),
                    )
                )
            starts.append(ring.owner(offset) * cols + (core ^ source) * half_cols)
    query_t, key_t, value_t, out_all = place_blocks(
        plan,
        [mine[0], theirs[0], mine[1], theirs[1]],
        starts,
        [(ranks * cols, edges[t + 1] - edges[t]) for t in range(4)],
    )

    inputs_own = wide(own_rows(after(tokens, theirs[1])))
    root_own = lax.rsqrt(jnp.mean(inputs_own * inputs_own, axis=-1, keepdims=True) + epsilon)
    normed_own = low(inputs_own * root_own * gain_attn)
    rank_ref = rank.astype(jnp.int32).reshape(1)
    groups = [
        (slice(j * width // 2, (j + 1) * width // 2), latent[:, j * inner : (j + 1) * inner])
        for j in range(2)
    ]
    queries = low(dot_last(normed_own, query_t))
    keys = [low(dot_last(latent_j, key_t[s])) for s, latent_j in groups]
    values = [low(dot_last(latent_j, value_t[s])) for s, latent_j in groups]
    queries, w1 = lax.optimization_barrier((queries, unit_ring.settle(queries, keys, values)))
    w2 = unit_ring.step()
    mixed, lse = attention_forward(rank_ref, ranks, queries, keys, values)
    w2 = unit_ring.settle(mixed)
    w3 = unit_ring.step()
    hidden = inputs_own + dot_plain(mixed, out_all)

    root_mlp = lax.rsqrt(jnp.mean(hidden * hidden, axis=-1, keepdims=True) + epsilon)
    normed_mlp = low(hidden * root_mlp * gain_mlp)
    unit_ring.settle(normed_mlp)
    normed_pair = flip(normed_mlp, members // 2)
    unit_ring.last_steps(normed_pair)
    blocks, _ = lax.optimization_barrier((unit_ring.blocks, normed_mlp))
    normed_mlp = dp_gather_rest(jnp.concatenate([normed_mlp, normed_pair], axis=0))
    units = jnp.concatenate([whole_block(blocks[o]) for o in offsets], axis=0)
    gate_t, up_t, down = units[:, :width], units[:, width : 2 * width], units[:, 2 * width :]
    gate = dot_last(normed_mlp, gate_t)
    up = dot_last(normed_mlp, up_t)
    logistic = jax.nn.sigmoid(gate)
    act = low(gate * logistic * up)
    grad_act = dot_last(grad_low_all, down)
    grad_gate = low(grad_act * up * logistic * (1.0 + gate * (1.0 - logistic)))
    grad_up = low(grad_act * gate * logistic)
    normed_part = low(dot_plain(grad_gate, gate_t) + dot_plain(grad_up, up_t))
    normed_sum = dp_scatter_step(normed_part, 1)
    mlp_sum = dp_scatter_step(after(low(dot_plain(act, down)), normed_sum), 1)
    grad_gate, grad_up, act, *_ = lax.optimization_barrier((grad_gate, grad_up, act, mlp_sum))
    grad_units = jnp.concatenate(
        [
            low(contract_rows(grad_gate, normed_mlp)),
            low(contract_rows(grad_up, normed_mlp)),
            low(contract_rows(act, grad_low_all)),
        ],
        axis=1,
    )

    def unit_rows(offset):
        spot = offsets.index(offset)
        return grad_units[spot * share : (spot + 1) * share]

    unit_sums = Scatter("mlp_grads", ring, unit_rows)
    r1 = unit_sums.step()

    def norm_backward(incoming, gain, entered, scale):
        scaled = gain * incoming
        inner_mean = jnp.mean(scaled * entered, axis=-1, keepdims=True)
        grad = scale * scaled - entered * (scale * scale * scale) * inner_mean
        return grad, jnp.sum(incoming * entered * scale, axis=0)

    incoming = wide(dp_scatter(normed_sum, 2, r1))
    grad_hidden, grad_gain_mlp = norm_backward(incoming, gain_mlp, hidden, root_mlp)
    grad_hidden = grad_out + grad_hidden
    grad_hidden_low = low(grad_hidden)
    r2 = unit_sums.step(grad_hidden_low)
    mlp_out = dp_scatter(after(mlp_sum, grad_hidden_low), 2)

    grad_mixed = low(dot_last(grad_hidden_low, out_all))
    pairs = width // (4 * HD)
    grads = [
        attention_backward(rank_ref, ranks, 0, queries, keys[0], values[0], mixed, grad_mixed, lse)
    ]
    r2 = unit_sums.settle(grads[0][0], mlp_out)
    grad_mixed, block_own, _ = lax.optimization_barrier((grad_mixed, low(hidden + mlp_out), r2))
    r3 = unit_sums.step()
    block_ring = Gather("block_out", ring, block_own)
    b1 = block_ring.step()
    grads.append(
        attention_backward(
            rank_ref, ranks, pairs, queries, keys[1], values[1], mixed, grad_mixed, lse
        )
    )
    r4 = unit_sums.step(grads[1][0], b1)
    grads, _ = lax.optimization_barrier((grads, unit_sums.given))
    grad_latent = [
        low(dot_plain(g[1], key_t[s]) + dot_plain(g[2], value_t[s]))
        for (s, _), g in zip(groups, grads)
    ]
    grad_latent = jnp.concatenate(grad_latent, axis=1)
    latent_sums = Scatter("latent_grads", ring, lambda o: own_rows(grad_latent, ring.owner(o)))
    edge = (*r4, *latent_sums.step())

    hidden_late, grads_late, _ = lax.optimization_barrier(
        (grad_hidden_low, grads, latent_sums.given)
    )
    hidden_cols = member_cols(hidden_late)
    grad_w_out = dp_scatter_cols_step(low(contract_rows(mixed, hidden_cols)), 1)
    inner_part = inner // members
    grad_w_kv = [
        jnp.concatenate(
            [low(contract_rows(latent_j, g[i])) for (_, latent_j), g in zip(groups, grads_late)],
            axis=1,
        )
        for i in (1, 2)
    ]
    kv = jnp.concatenate(
        [
            lax.dynamic_slice_in_dim(g, (member ^ r) * inner_part, inner_part, 0)
            for r in order
            for g in grad_w_kv
        ],
        axis=0,
    )
    kv = dp_scatter_step(kv, 1)
    normed_cols = member_cols(normed_own)
    grad_w_query = jnp.concatenate([g[0] for g in grads_late], axis=1)
    grad_w_query = low(contract_rows(grad_w_query, normed_cols))
    for step in range(ring.half - 1):
        if step == 1:
            edge = (edge, grad_w_out, kv)
            grad_w_out, kv = dp_scatter_cols(grad_w_out, 2), dp_scatter(kv, 2)
            grad_w_query = dp_scatter_cols_step(grad_w_query, 1)
        if step == 2:
            edge = (edge, grad_w_out, kv, grad_w_query)
            grad_w_query = dp_scatter_cols(grad_w_query, 2)
        edge = (*latent_sums.step(*edge), *block_ring.step(*edge))
    block_ring.last_steps()
    grad_latent_own = low(latent_sums.last_steps())
    grad_normed = dot_last(grad_latent_own, w_latent)
    for (s, _), g in zip(groups, grads):
        grad_normed += dot_plain(g[0], query_t[s])
    grad_inputs, grad_gain_attn = norm_backward(grad_normed, gain_attn, inputs_own, root_own)
    gain_rows = jnp.stack([low(grad_gain_attn), low(grad_gain_mlp)])
    gain_rows = jnp.concatenate([gain_rows, jnp.zeros((14, width), jnp.bfloat16)], axis=0)
    token_ring = Gather(
        "grad_tokens",
        ring,
        jnp.concatenate([low(grad_hidden + grad_inputs), gain_rows], axis=0),
    )
    edge = token_ring.step(*block_ring.edge)
    unit_sums.settle(*edge)
    mlp_grads = low(unit_sums.last_steps())
    mlp_grads = jnp.concatenate(
        [
            jnp.concatenate(
                [mlp_grads[:, w * width + m * part : w * width + (m + 1) * part] for w in range(3)],
                axis=1,
            )
            for m in range(members)
        ],
        axis=0,
    )
    grad_w_latent = low(contract_rows(grad_latent_own, normed_cols))
    grad_w_latent = dp_scatter_cols(grad_w_latent)
    latent_cols = w_latent.shape[1] // ranks
    side_by_side = 2 * cols == part

    def attn_block(offset):
        of = ring.owner(offset)
        kv_piece = lax.dynamic_slice_in_dim(kv, of * cols, cols, 1)
        if side_by_side:
            kv_piece = jnp.concatenate([kv_piece[:inner_part], kv_piece[inner_part:]], axis=1)
        return jnp.concatenate(
            [
                lax.dynamic_slice_in_dim(grad_w_out, of * cols, cols, 0),
                lax.dynamic_slice_in_dim(grad_w_query, of * cols, cols, 0),
                lax.dynamic_slice_in_dim(grad_w_latent, of * latent_cols, latent_cols, 0),
                kv_piece.reshape(-1, part),
            ],
            axis=0,
        )

    attn_sums = Scatter("attn_grads", ring, attn_block)
    for step in range(ring.half - 1):
        edge = (*token_ring.step(*edge), *attn_sums.step(*edge))
        if step == 0:
            mlp_grads = lax.all_to_all(after(mlp_grads, edge), "dp", 0, 0, tiled=True)
        if step == 1:
            mlp_grads, blocks, _ = lax.optimization_barrier((mlp_grads, block_ring.blocks, edge))
            mlp_grads, block_out = wide(mlp_grads), place_rows(blocks)
    attn_grads = attn_sums.last_steps(*edge)
    kv_grads = attn_grads[2 * cols + latent_cols :]
    if side_by_side:
        kv_grads = kv_grads[:, :cols], kv_grads[:, cols:]
    else:
        kv_grads = kv_grads.reshape(2, inner_part, cols)
    grad_tokens = place_rows(token_ring.last_steps())

    gains = sum(
        wide(whole_block(piece)[2 * block : 2 * block + 2]) for piece in token_ring.blocks.values()
    )
    gains = jnp.stack(
        [lax.dynamic_slice_in_dim(gains, (member ^ r) * part, part, 1) for r in order]
    )
    gains = dp_sum_blocks(gains)[0]
    return (
        block_out,
        grad_tokens,
        gains[0],
        attn_grads[cols : 2 * cols].T,
        attn_grads[2 * cols : 2 * cols + latent_cols].T,
        kv_grads[0],
        kv_grads[1],
        attn_grads[:cols],
        gains[1],
        mlp_grads[:, :part].T,
        mlp_grads[:, part : 2 * part].T,
        mlp_grads[:, 2 * part :],
    )


def solution(mesh):
    in_specs = (
        P("dp", None),
        P("dp", None),
        P("dp"),
        P(),
        P(),
        P(None, "head"),
        P(),
        P(None, "head"),
        P(None, "head"),
        P("head", None),
        P(),
        P(None, "head"),
        P(None, "head"),
        P("head", None),
    )
    out_specs = (
        P("dp", None),
        P("dp", None),
        P("dp"),
        P("dp", "head"),
        P("dp", "head"),
        P("dp", "head"),
        P("dp", "head"),
        P("head", "dp"),
        P("dp"),
        P("dp", "head"),
        P("dp", "head"),
        P("head", "dp"),
    )
    return jax.shard_map(body, mesh=mesh, in_specs=in_specs, out_specs=out_specs, check_vma=False)
```

```python
import functools

import jax
import jax.numpy as jnp
from jax import lax
from jax.experimental import pallas as pl
from jax.experimental.pallas import tpu as pltpu
from jax.sharding import PartitionSpec as P

HD = 64
epsilon = 1e-05
negative = -1e30


def snake_order(count):
    return list(range(0, count, 2)) + list(range(count - 1, 0, -2))


def after(block, *earlier):
    return lax.optimization_barrier((block, earlier))[0] if earlier else block


class Ring:
    def __init__(self):
        self.count = lax.axis_size("head")
        self.half = self.count // 2
        order = snake_order(self.count)
        self.forward = [(order[i], order[(i + 1) % self.count]) for i in range(self.count)]
        self.backward = [(b, a) for a, b in self.forward]
        index = lax.axis_index("head")
        self.place = jnp.where(index % 2 == 0, index // 2, self.count - 1 - index // 2)
        self.offsets = [0]
        for step in range(1, self.half):
            self.offsets += [-step, step]
        self.offsets.append(self.half)

    def owner(self, offset):
        spot = (self.place + offset) % self.count
        return jnp.where(spot < self.half, 2 * spot, 2 * (self.count - 1 - spot) + 1)

    def send(self, name, ahead, behind):
        with jax.named_scope(name):
            return (
                lax.ppermute(ahead, "head", self.forward),
                lax.ppermute(behind, "head", self.backward),
            )


class Gather:
    def __init__(self, name, ring, own):
        self.name, self.ring, self.blocks, self.taken = name, ring, {0: own}, 0
        self.edge = (own, own)

    def settle(self, *gates):
        *self.edge, _ = lax.optimization_barrier((*self.edge, gates))
        if 0 < self.taken < self.ring.half:
            self.blocks[-self.taken], self.blocks[self.taken] = self.edge
        elif self.taken:
            self.blocks[self.taken] = tuple(self.edge)
        return self.edge

    def step(self, *gates):
        self.settle(*gates)
        self.taken += 1
        ahead, behind = self.given = tuple(self.edge)
        if self.taken == self.ring.half:
            cut = ahead.shape[-1] // 2
            self.edge = self.ring.send(self.name, ahead[..., :cut], behind[..., cut:])
            self.blocks[self.taken] = self.edge
        else:
            self.edge = self.ring.send(self.name, ahead, behind)
            self.blocks[-self.taken], self.blocks[self.taken] = self.edge
        return self.edge

    def last_steps(self, *gates):
        while self.taken < self.ring.half:
            self.step(*gates)
            gates = ()
        return self.blocks


class Scatter:
    def __init__(self, name, ring, block):
        self.name, self.ring, self.block, self.taken = name, ring, block, 0

    def step(self, *gates):
        left = self.ring.half - self.taken
        if self.taken == 0:
            far = after(self.block(left), *gates)
            cut = far.shape[-1] // 2
            give = far[..., :cut], far[..., cut:]
        else:
            give = self.block(left), self.block(-left)
            ahead, behind, _ = lax.optimization_barrier((*self.edge, gates))
            cut = ahead.shape[-1]
            if self.taken == 1:
                give = (
                    jnp.concatenate([add(give[0][..., :cut], ahead), give[0][..., cut:]], axis=-1),
                    jnp.concatenate([give[1][..., :cut], add(give[1][..., cut:], behind)], axis=-1),
                )
            else:
                give = add(give[0], ahead), add(give[1], behind)
        self.taken, self.given = self.taken + 1, give
        self.edge = self.ring.send(self.name, *give)
        return self.edge

    def settle(self, *gates):
        *self.edge, _ = lax.optimization_barrier((*self.edge, gates))
        return self.edge

    def last_steps(self, *gates):
        while self.taken < self.ring.half:
            self.step(*gates)
            gates = ()
        return wide(self.block(0)) + wide(self.edge[0]) + wide(self.edge[1])


def whole_block(piece):
    return jnp.concatenate(piece, axis=-1) if isinstance(piece, tuple) else piece


def stack_blocks(blocks, offsets):
    return jnp.concatenate([whole_block(blocks[o]) for o in offsets], axis=0)


def copy_kernel(plan, sources, starts_ref, *refs):
    inputs, outputs, sems = refs[:sources], refs[sources:-1], refs[-1]
    copies = []
    for i, (source, rows, cols, target, slot, target_cols) in enumerate(plan):
        count = rows[1] - rows[0]
        start = pl.multiple_of(starts_ref[slot], count)
        copies.append(
            pltpu.make_async_copy(
                inputs[source].at[rows[0] : rows[1], cols[0] : cols[1]],
                outputs[target].at[pl.ds(start, count), target_cols[0] : target_cols[1]],
                sems.at[i],
            )
        )
    for copy in copies:
        copy.start()
    for copy in copies:
        copy.wait()


def place_blocks(plan, arrays, starts, shapes):
    anywhere = pl.BlockSpec(memory_space=pl.ANY)
    return pl.pallas_call(
        functools.partial(copy_kernel, plan, len(arrays)),
        in_specs=[pl.BlockSpec(memory_space=pltpu.SMEM)]
        + [pl.BlockSpec(memory_space=pltpu.VMEM)] * len(arrays),
        out_specs=[anywhere] * len(shapes),
        out_shape=[jax.ShapeDtypeStruct(s, arrays[0].dtype) for s in shapes],
        scratch_shapes=[pltpu.SemaphoreType.DMA((len(plan),))],
        compiler_params=pltpu.CompilerParams(vmem_limit_bytes=20 * 2**20),
        cost_estimate=pl.CostEstimate(flops=0, bytes_accessed=0, transcendentals=0),
        name="place_blocks",
    )(jnp.stack(starts).astype(jnp.int32), *arrays)


def wide(block):
    return block.astype(jnp.float32)


def add(left, right):
    return (wide(left) + wide(right)).astype(jnp.bfloat16)


def flip(block, bit):
    count = lax.axis_size("dp")
    return lax.ppermute(block, "dp", [(i, i ^ bit) for i in range(count)])


def dp_bits():
    return lax.axis_size("dp").bit_length() - 1


def dp_gather(own, *gates):
    for bit, gate in zip(reversed(range(dp_bits())), (*gates, *[()] * dp_bits())):
        got = flip(own, 1 << bit)
        own, got, _ = lax.optimization_barrier((own, got, gate))
        own = jnp.concatenate([own, got], axis=0)
    return own


def dp_gather_rest(own):
    for bit in reversed(range(dp_bits() - 1)):
        own = jnp.concatenate([own, flip(own, 1 << bit)], axis=0)
    return own


def dp_bit_order():
    order = [0]
    for bit in reversed(range(dp_bits())):
        order = order + [r | 1 << bit for r in order]
    return order


def dp_scatter_step(blocks, distance, *gates):
    half = blocks.shape[0] // 2
    return add(blocks[:half], after(flip(blocks[half:], distance), *gates))


def dp_scatter(blocks, distance=1, *gates):
    while distance < lax.axis_size("dp"):
        blocks = dp_scatter_step(blocks, distance, *gates)
        distance *= 2
    return blocks


def dp_scatter_cols_step(blocks, distance):
    half = blocks.shape[1] // 2
    return add(blocks[:, :half], flip(blocks[:, half:], distance))


def dp_scatter_cols(blocks, distance=1):
    while distance < lax.axis_size("dp"):
        blocks = dp_scatter_cols_step(blocks, distance)
        distance *= 2
    return blocks


def dp_sum_blocks(blocks):
    distance = 1
    while distance < lax.axis_size("dp"):
        half = blocks.shape[0] // 2
        blocks = blocks[:half] + flip(blocks[half:], distance)
        distance *= 2
    return blocks


def dot_last(a, b):
    return lax.dot_general(a, b, (((1,), (1,)), ((), ())), preferred_element_type=jnp.float32)

def dot_plain(a, b):
    return jnp.dot(a, b, preferred_element_type=jnp.float32)

def lane_heads(x, e):
    lane = lax.broadcasted_iota(jnp.int32, x.shape, 1)
    return jnp.where(lane // HD == e, x, jnp.zeros_like(x))

def segments(length, block):
    half = length // 2
    if block % 128 == 0:
        return ((0, half, 0, 2 * block, block), (half, length, block, 2 * block, block))
    return ((0, half, 0, 2 * block, 2 * block), (half, length, 0, 2 * block, 2 * block))

def visible(first_key, count, first_col, cols, block, rank, ranks):
    key = first_key + lax.broadcasted_iota(jnp.int32, (count, cols), 0)
    col = first_col + lax.broadcasted_iota(jnp.int32, (count, cols), 1)
    row = jnp.where(col < block, rank * block + col, (ranks - 1 + rank) * block + col)
    return key <= row

def fwd_heads(ranks, rank_ref, q_ref, k_ref, v_ref, o_ref, lse_ref):
    length = k_ref.shape[0]
    block = q_ref.shape[0] // 2
    rank = rank_ref[0]
    heads = q_ref.shape[1] // HD
    query = q_ref[...]
    value_t = v_ref[...].T
    queries = [lane_heads(query, e) * jnp.bfloat16(HD**-0.5) for e in range(heads)]
    parts = segments(length, block)
    scores = [[] for _ in range(heads)]
    peaks = [jnp.full((1, 2 * block), negative, jnp.float32) for _ in range(heads)]
    for k0, k1, c0, c1, masked in parts:
        keep = visible(k0, k1 - k0, c0, masked, block, rank, ranks)
        for e in range(heads):
            s = dot_last(k_ref[k0:k1, :], queries[e][c0:c1, :])
            if masked == c1 - c0:
                s = jnp.where(keep, s, negative)
            else:
                s = jnp.concatenate([jnp.where(keep, s[:, :masked], negative), s[:, masked:]], axis=1)
            top = jnp.max(s, axis=0, keepdims=True)
            if c0:
                top = jnp.concatenate([jnp.full((1, c0), negative, jnp.float32), top], axis=1)
            peaks[e] = jnp.maximum(peaks[e], top)
            scores[e].append(s)
    totals = [jnp.zeros((1, 2 * block), jnp.float32) for _ in range(heads)]
    mixed = [jnp.zeros((q_ref.shape[1], 2 * block), jnp.float32) for _ in range(heads)]
    for i, (k0, k1, c0, c1, masked) in enumerate(parts):
        for e in range(heads):
            w = jnp.exp(scores[e][i] - peaks[e][:, c0:c1])
            part = jnp.sum(w, axis=0, keepdims=True)
            m = dot_plain(value_t[:, k0:k1], w.astype(jnp.bfloat16))
            if c0:
                part = jnp.concatenate([jnp.zeros((1, c0), jnp.float32), part], axis=1)
                m = jnp.concatenate([jnp.zeros((m.shape[0], c0), jnp.float32), m], axis=1)
            totals[e] += part
            mixed[e] += m
    outs = [mixed[e][e * HD:(e + 1) * HD] / totals[e] for e in range(heads)]
    o_ref[...] = jnp.concatenate(outs, axis=0).T.astype(o_ref.dtype)
    lses = [peaks[e] + jnp.log(totals[e]) for e in range(heads)]
    lse_ref[0] = jnp.concatenate(lses + [jnp.zeros((8 - heads, 2 * block), jnp.float32)], axis=0)


def fwd_kernel(ranks, split, rank_ref, q_ref, *refs):
    keys, values, outs = refs[:2], refs[2:4], refs[4:]
    for j in range(2):

        @pl.when(pl.program_id(0) // split == j)
        def _():
            fwd_heads(ranks, rank_ref, q_ref, keys[j], values[j], *outs)


def attention_forward(rank, ranks, query, keys, values):
    rows, width = query.shape
    length = keys[0].shape[0]
    lanes = 2 * HD
    pairs = width // lanes
    split = pairs // 2
    key_specs = [
        pl.BlockSpec((length, lanes), lambda i: (0, jnp.minimum(i, split - 1))),
        pl.BlockSpec((length, lanes), lambda i: (0, jnp.maximum(i - split, 0))),
    ]
    return pl.pallas_call(
        functools.partial(fwd_kernel, ranks, split),
        grid=(pairs,),
        in_specs=[
            pl.BlockSpec(memory_space=pltpu.SMEM),
            pl.BlockSpec((rows, lanes), lambda i: (0, i)),
            *key_specs,
            *key_specs,
        ],
        out_specs=[
            pl.BlockSpec((rows, lanes), lambda i: (0, i)),
            pl.BlockSpec((1, 8, rows), lambda i: (i, 0, 0)),
        ],
        out_shape=[
            jax.ShapeDtypeStruct((rows, width), jnp.bfloat16),
            jax.ShapeDtypeStruct((pairs, 8, rows), jnp.float32),
        ],
        compiler_params=pltpu.CompilerParams(vmem_limit_bytes=20 * 2**20),
        cost_estimate=pl.CostEstimate(flops=0, bytes_accessed=0, transcendentals=0),
        name="attention_forward",
    )(rank, query, *keys, *values)


def bwd_kernel(ranks, step, rank_ref, q_ref, k_ref, v_ref, o_ref, g_ref, lse_ref, dq_ref, dk_ref, dv_ref):
    length = k_ref.shape[0]
    block = q_ref.shape[0] // 2
    rank = rank_ref[0]
    heads = q_ref.shape[1] // HD
    query, grad = q_ref[...], g_ref[...]
    key_t = k_ref[...].T
    spread = (grad.astype(jnp.float32) * o_ref[...].astype(jnp.float32)).T
    queries = [lane_heads(query, e) * jnp.bfloat16(HD**-0.5) for e in range(heads)]
    grads = [lane_heads(grad, e) for e in range(heads)]
    deltas = [jnp.sum(spread[e * HD:(e + 1) * HD], axis=0, keepdims=True) for e in range(heads)]
    dq = [jnp.zeros((q_ref.shape[1], 2 * block), jnp.float32) for e in range(heads)]
    for k0, k1, c0, c1, masked in segments(length, block):
        for s0 in range(k0, k1, step):
            k_c, v_c = k_ref[s0:s0 + step, :], v_ref[s0:s0 + step, :]
            keep = visible(s0, step, c0, masked, block, rank, ranks)
            dk = jnp.zeros((step, q_ref.shape[1]), jnp.float32)
            dv = jnp.zeros((step, q_ref.shape[1]), jnp.float32)
            for e in range(heads):
                s = dot_last(k_c, queries[e][c0:c1, :])
                p = jnp.exp(s - lse_ref[0, e:e + 1, c0:c1])
                if masked == c1 - c0:
                    p = jnp.where(keep, p, 0.0)
                else:
                    p = jnp.concatenate([jnp.where(keep, p[:, :masked], 0.0), p[:, masked:]], axis=1)
                dp = dot_last(v_c, grads[e][c0:c1, :])
                ds = (p * (dp - deltas[e][:, c0:c1])).astype(jnp.bfloat16)
                dv += dot_plain(p.astype(jnp.bfloat16), grads[e][c0:c1, :])
                dk += dot_plain(ds, queries[e][c0:c1, :])
                m = dot_plain(key_t[:, s0:s0 + step], ds)
                if c0:
                    m = jnp.concatenate([jnp.zeros((m.shape[0], c0), jnp.float32), m], axis=1)
                dq[e] += m
            dk_ref[s0:s0 + step, :] = dk.astype(jnp.bfloat16)
            dv_ref[s0:s0 + step, :] = dv.astype(jnp.bfloat16)
    own = jnp.concatenate([dq[e][e * HD:(e + 1) * HD] for e in range(heads)], axis=0)
    dq_ref[...] = (own * HD**-0.5).T.astype(jnp.bfloat16)

def attention_backward(rank, ranks, first, query, key, value, mixed, grad, lse, step=512):
    rows = query.shape[0]
    length, width = key.shape
    lanes = 2 * HD
    pairs = width // lanes
    row_spec = pl.BlockSpec((rows, lanes), lambda i: (0, i + first))
    key_spec = pl.BlockSpec((length, lanes), lambda i: (0, i))
    return pl.pallas_call(
        functools.partial(bwd_kernel, ranks, step),
        grid=(pairs,),
        in_specs=[
            pl.BlockSpec(memory_space=pltpu.SMEM),
            row_spec, key_spec, key_spec, row_spec, row_spec,
            pl.BlockSpec((1, 8, rows), lambda i: (i + first, 0, 0)),
        ],
        out_specs=[pl.BlockSpec((rows, lanes), lambda i: (0, i)), key_spec, key_spec],
        out_shape=[
            jax.ShapeDtypeStruct((rows, width), jnp.bfloat16),
            jax.ShapeDtypeStruct((length, width), jnp.bfloat16),
            jax.ShapeDtypeStruct((length, width), jnp.bfloat16),
        ],
        compiler_params=pltpu.CompilerParams(vmem_limit_bytes=20 * 2**20),
        cost_estimate=pl.CostEstimate(flops=0, bytes_accessed=0, transcendentals=0),
        name="attention_backward",
    )(rank, query, key, value, mixed, grad, lse)

def contract_rows(left, right):
    return lax.dot_general(
        left, right, (((0,), (0,)), ((), ())), preferred_element_type=jnp.float32
    )


def low(block):
    return block.astype(jnp.bfloat16)


def body(
    tokens,
    cotangent,
    group_ids,
    group_weights,
    gain_attn,
    w_query,
    w_latent,
    w_key,
    w_value,
    w_out,
    gain_mlp,
    w_gate,
    w_up,
    w_down,
):
    ring = Ring()
    ranks, members = ring.count, lax.axis_size("dp")
    rank, member = lax.axis_index("head"), lax.axis_index("dp")
    length, width = tokens.shape
    block = length // (2 * ranks)
    cols = w_query.shape[1]
    inner = w_key.shape[0]
    share = w_gate.shape[1] // members
    part = width // members
    order = dp_bit_order()
    offsets = ring.offsets

    def own_rows(whole, of=None):
        of = rank if of is None else of
        first = lax.dynamic_slice_in_dim(whole, of * block, block, 0)
        second = lax.dynamic_slice_in_dim(whole, (ranks + of) * block, block, 0)
        return jnp.concatenate([first, second], axis=0)

    def place_rows(blocks):
        plan, arrays, starts = [], [], []
        for offset, piece in blocks.items():
            of = ring.owner(offset)
            first = 0
            for array in piece if isinstance(piece, tuple) else (piece,):
                last = first + array.shape[1]
                for slot in range(2):
                    plan.append(
                        (
                            len(arrays),
                            (slot * block, (slot + 1) * block),
                            (0, array.shape[1]),
                            0,
                            len(starts) + slot,
                            (first, last),
                        )
                    )
                arrays.append(array)
                first = last
            starts += [of * block, (ranks + of) * block]
        return place_blocks(plan, arrays, starts, [(length, width)])[0]

    def member_cols(whole):
        return jnp.concatenate(
            [lax.dynamic_slice_in_dim(whole, (member ^ r) * part, part, 1) for r in order], axis=1
        )

    core = member % 2
    packed = jnp.concatenate([w_query.T, w_key.T, w_value.T, w_out], axis=1)
    half_cols = cols // 2
    attn_ring = Gather("attn_weights", ring, lax.dynamic_slice_in_dim(packed, core * half_cols, half_cols, 0))
    a1 = attn_ring.step()
    inputs = wide(tokens)
    root = lax.rsqrt(jnp.mean(inputs * inputs, axis=-1, keepdims=True) + epsilon)
    normed = low(inputs * root * gain_attn)
    a2 = attn_ring.step(normed)
    labels = jnp.arange(group_weights.shape[0], dtype=jnp.int32)
    row_weight = jnp.sum(jnp.where(group_ids[0] == labels, group_weights, 0.0))
    grad_out = wide(own_rows(cotangent)) * row_weight
    grad_low = low(grad_out)
    grad_low_pair = flip(grad_low, members // 2)
    latent = low(dot_plain(after(normed, *a1), w_latent))

    grad_low_pair, latent, _ = lax.optimization_barrier((grad_low_pair, latent, attn_ring.settle(latent)))
    a3 = attn_ring.step(grad_low_pair)
    grad_low_all = dp_gather_rest(jnp.concatenate([grad_low, grad_low_pair], axis=0))

    gate_w, up_w, down_w, *_ = lax.optimization_barrier((w_gate, w_up, w_down, *a2))
    units = jnp.concatenate(
        [
            lax.dynamic_slice_in_dim(gate_w, member * share, share, 1).T,
            lax.dynamic_slice_in_dim(up_w, member * share, share, 1).T,
            lax.dynamic_slice_in_dim(down_w, member * share, share, 0),
        ],
        axis=1,
    )
    early = [0, -1, 1, -2, 2] if ring.half > 3 else [0]
    mine = [stack_blocks(attn_ring.blocks, early)]
    theirs = [flip(mine[0], 1)]
    attn_ring.step(units, grad_low_all, theirs[0])
    unit_ring = Gather("mlp_weights", ring, units)
    w1 = unit_ring.step(*a3)

    blocks = attn_ring.last_steps()
    late = [o for o in offsets if o not in early]
    mine.append(stack_blocks(blocks, late))
    theirs.append(flip(mine[1], 1))
    edges = (0, width, width + inner, width + 2 * inner, 2 * width + 2 * inner)
    plan, starts = [], []
    for spot, offset in enumerate(early + late):
        bundle = int(spot >= len(early))
        row = (spot - bundle * len(early)) * half_cols
        for source in range(2):
            for target in range(4):
                plan.append(
                    (
                        2 * bundle + source,
                        (row, row + half_cols),
                        (edges[target], edges[target + 1]),
                        target,
                        len(starts),
                        (0, edges[target + 1] - edges[target]),
                    )
                )
            starts.append(ring.owner(offset) * cols + (core ^ source) * half_cols)
    query_t, key_t, value_t, out_all = place_blocks(
        plan,
        [mine[0], theirs[0], mine[1], theirs[1]],
        starts,
        [(ranks * cols, edges[t + 1] - edges[t]) for t in range(4)],
    )

    inputs_own = wide(own_rows(after(tokens, theirs[1])))
    root_own = lax.rsqrt(jnp.mean(inputs_own * inputs_own, axis=-1, keepdims=True) + epsilon)
    normed_own = low(inputs_own * root_own * gain_attn)
    rank_ref = rank.astype(jnp.int32).reshape(1)
    groups = [
        (slice(j * width // 2, (j + 1) * width // 2), latent[:, j * inner : (j + 1) * inner])
        for j in range(2)
    ]
    queries = low(dot_last(normed_own, query_t))
    keys = [low(dot_last(latent_j, key_t[s])) for s, latent_j in groups]
    values = [low(dot_last(latent_j, value_t[s])) for s, latent_j in groups]
    queries, w1 = lax.optimization_barrier((queries, unit_ring.settle(queries, keys, values)))
    w2 = unit_ring.step()
    mixed, lse = attention_forward(rank_ref, ranks, queries, keys, values)
    w2 = unit_ring.settle(mixed)
    w3 = unit_ring.step()
    hidden = inputs_own + dot_plain(mixed, out_all)

    root_mlp = lax.rsqrt(jnp.mean(hidden * hidden, axis=-1, keepdims=True) + epsilon)
    normed_mlp = low(hidden * root_mlp * gain_mlp)
    unit_ring.settle(normed_mlp)
    normed_pair = flip(normed_mlp, members // 2)
    unit_ring.last_steps(normed_pair)
    blocks, _ = lax.optimization_barrier((unit_ring.blocks, normed_mlp))
    normed_mlp = dp_gather_rest(jnp.concatenate([normed_mlp, normed_pair], axis=0))
    units = jnp.concatenate([whole_block(blocks[o]) for o in offsets], axis=0)
    gate_t, up_t, down = units[:, :width], units[:, width : 2 * width], units[:, 2 * width :]
    gate = dot_last(normed_mlp, gate_t)
    up = dot_last(normed_mlp, up_t)
    logistic = jax.nn.sigmoid(gate)
    act = low(gate * logistic * up)
    grad_act = dot_last(grad_low_all, down)
    grad_gate = low(grad_act * up * logistic * (1.0 + gate * (1.0 - logistic)))
    grad_up = low(grad_act * gate * logistic)
    normed_part = low(dot_plain(grad_gate, gate_t) + dot_plain(grad_up, up_t))
    normed_sum = dp_scatter_step(normed_part, 1)
    mlp_sum = dp_scatter_step(after(low(dot_plain(act, down)), normed_sum), 1)
    grad_gate, grad_up, act, *_ = lax.optimization_barrier((grad_gate, grad_up, act, mlp_sum))
    grad_units = jnp.concatenate(
        [
            low(contract_rows(grad_gate, normed_mlp)),
            low(contract_rows(grad_up, normed_mlp)),
            low(contract_rows(act, grad_low_all)),
        ],
        axis=1,
    )

    def unit_rows(offset):
        spot = offsets.index(offset)
        return grad_units[spot * share : (spot + 1) * share]

    unit_sums = Scatter("mlp_grads", ring, unit_rows)
    r1 = unit_sums.step()

    def norm_backward(incoming, gain, entered, scale):
        scaled = gain * incoming
        inner_mean = jnp.mean(scaled * entered, axis=-1, keepdims=True)
        grad = scale * scaled - entered * (scale * scale * scale) * inner_mean
        return grad, jnp.sum(incoming * entered * scale, axis=0)

    incoming = wide(dp_scatter(normed_sum, 2, r1))
    grad_hidden, grad_gain_mlp = norm_backward(incoming, gain_mlp, hidden, root_mlp)
    grad_hidden = grad_out + grad_hidden
    grad_hidden_low = low(grad_hidden)
    r2 = unit_sums.step(grad_hidden_low)
    mlp_out = dp_scatter(after(mlp_sum, grad_hidden_low), 2)

    grad_mixed = low(dot_last(grad_hidden_low, out_all))
    pairs = width // (4 * HD)
    grads = [
        attention_backward(rank_ref, ranks, 0, queries, keys[0], values[0], mixed, grad_mixed, lse)
    ]
    r2 = unit_sums.settle(grads[0][0], mlp_out)
    grad_mixed, block_own, _ = lax.optimization_barrier((grad_mixed, low(hidden + mlp_out), r2))
    r3 = unit_sums.step()
    block_ring = Gather("block_out", ring, block_own)
    b1 = block_ring.step()
    grads.append(
        attention_backward(
            rank_ref, ranks, pairs, queries, keys[1], values[1], mixed, grad_mixed, lse
        )
    )
    r4 = unit_sums.step(grads[1][0], b1)
    grads, _ = lax.optimization_barrier((grads, unit_sums.given))
    grad_latent = [
        low(dot_plain(g[1], key_t[s]) + dot_plain(g[2], value_t[s]))
        for (s, _), g in zip(groups, grads)
    ]
    grad_latent = jnp.concatenate(grad_latent, axis=1)
    latent_sums = Scatter("latent_grads", ring, lambda o: own_rows(grad_latent, ring.owner(o)))
    edge = (*r4, *latent_sums.step())

    hidden_late, grads_late, _ = lax.optimization_barrier(
        (grad_hidden_low, grads, latent_sums.given)
    )
    hidden_cols = member_cols(hidden_late)
    grad_w_out = dp_scatter_cols_step(low(contract_rows(mixed, hidden_cols)), 1)
    inner_part = inner // members
    grad_w_kv = [
        jnp.concatenate(
            [low(contract_rows(latent_j, g[i])) for (_, latent_j), g in zip(groups, grads_late)],
            axis=1,
        )
        for i in (1, 2)
    ]
    kv = jnp.concatenate(
        [
            lax.dynamic_slice_in_dim(g, (member ^ r) * inner_part, inner_part, 0)
            for r in order
            for g in grad_w_kv
        ],
        axis=0,
    )
    kv = dp_scatter_step(kv, 1)
    normed_cols = member_cols(normed_own)
    grad_w_query = jnp.concatenate([g[0] for g in grads_late], axis=1)
    grad_w_query = low(contract_rows(grad_w_query, normed_cols))
    for step in range(ring.half - 1):
        if step == 1:
            edge = (edge, grad_w_out, kv)
            grad_w_out, kv = dp_scatter_cols(grad_w_out, 2), dp_scatter(kv, 2)
            grad_w_query = after(grad_w_query, latent_sums.given)
            grad_w_query = dp_scatter_cols_step(grad_w_query, 1)
        if step == 2:
            edge = (edge, grad_w_out, kv, grad_w_query)
            grad_w_query = dp_scatter_cols(grad_w_query, 2)
        edge = (*latent_sums.step(*edge), *block_ring.step(*edge))
    block_ring.last_steps()
    grad_latent_own = low(latent_sums.last_steps())
    grad_normed = dot_last(grad_latent_own, w_latent)
    for (s, _), g in zip(groups, grads):
        grad_normed += dot_plain(g[0], query_t[s])
    grad_inputs, grad_gain_attn = norm_backward(grad_normed, gain_attn, inputs_own, root_own)
    gain_rows = jnp.stack([low(grad_gain_attn), low(grad_gain_mlp)])
    gain_rows = jnp.concatenate([gain_rows, jnp.zeros((14, width), jnp.bfloat16)], axis=0)
    token_ring = Gather(
        "grad_tokens",
        ring,
        jnp.concatenate([low(grad_hidden + grad_inputs), gain_rows], axis=0),
    )
    edge = token_ring.step(*block_ring.edge)
    unit_sums.settle(*edge)
    mlp_grads = low(unit_sums.last_steps())
    mlp_grads = jnp.concatenate(
        [
            jnp.concatenate(
                [mlp_grads[:, w * width + m * part : w * width + (m + 1) * part] for w in range(3)],
                axis=1,
            )
            for m in range(members)
        ],
        axis=0,
    )
    grad_w_latent = low(contract_rows(grad_latent_own, normed_cols))
    grad_w_latent = dp_scatter_cols(grad_w_latent)
    latent_cols = w_latent.shape[1] // ranks
    side_by_side = 2 * cols == part

    def attn_block(offset):
        of = ring.owner(offset)
        kv_piece = lax.dynamic_slice_in_dim(kv, of * cols, cols, 1)
        if side_by_side:
            kv_piece = jnp.concatenate([kv_piece[:inner_part], kv_piece[inner_part:]], axis=1)
        return jnp.concatenate(
            [
                lax.dynamic_slice_in_dim(grad_w_out, of * cols, cols, 0),
                lax.dynamic_slice_in_dim(grad_w_query, of * cols, cols, 0),
                lax.dynamic_slice_in_dim(grad_w_latent, of * latent_cols, latent_cols, 0),
                kv_piece.reshape(-1, part),
            ],
            axis=0,
        )

    attn_sums = Scatter("attn_grads", ring, attn_block)
    for step in range(ring.half - 1):
        edge = (*token_ring.step(*edge), *attn_sums.step(*edge))
        if step == 0:
            mlp_grads = lax.all_to_all(after(mlp_grads, edge), "dp", 0, 0, tiled=True)
        if step == 1:
            mlp_grads, blocks, _ = lax.optimization_barrier((mlp_grads, block_ring.blocks, edge))
            mlp_grads, block_out = wide(mlp_grads), place_rows(blocks)
    attn_grads = attn_sums.last_steps(*edge)
    kv_grads = attn_grads[2 * cols + latent_cols :]
    if side_by_side:
        kv_grads = kv_grads[:, :cols], kv_grads[:, cols:]
    else:
        kv_grads = kv_grads.reshape(2, inner_part, cols)
    grad_tokens = place_rows(token_ring.last_steps())

    gains = sum(
        wide(whole_block(piece)[2 * block : 2 * block + 2]) for piece in token_ring.blocks.values()
    )
    gains = jnp.stack(
        [lax.dynamic_slice_in_dim(gains, (member ^ r) * part, part, 1) for r in order]
    )
    gains = dp_sum_blocks(gains)[0]
    return (
        block_out,
        grad_tokens,
        gains[0],
        attn_grads[cols : 2 * cols].T,
        attn_grads[2 * cols : 2 * cols + latent_cols].T,
        kv_grads[0],
        kv_grads[1],
        attn_grads[:cols],
        gains[1],
        mlp_grads[:, :part].T,
        mlp_grads[:, part : 2 * part].T,
        mlp_grads[:, 2 * part :],
    )


def solution(mesh):
    in_specs = (
        P("dp", None),
        P("dp", None),
        P("dp"),
        P(),
        P(),
        P(None, "head"),
        P(),
        P(None, "head"),
        P(None, "head"),
        P("head", None),
        P(),
        P(None, "head"),
        P(None, "head"),
        P("head", None),
    )
    out_specs = (
        P("dp", None),
        P("dp", None),
        P("dp"),
        P("dp", "head"),
        P("dp", "head"),
        P("dp", "head"),
        P("dp", "head"),
        P("head", "dp"),
        P("dp"),
        P("dp", "head"),
        P("dp", "head"),
        P("head", "dp"),
    )
    return jax.shard_map(body, mesh=mesh, in_specs=in_specs, out_specs=out_specs, check_vma=False)
```
